32 devices in a mesh: gx: 8 (over y, x, core), gz: 4 (over z).
Axes of the slice: x: 2, y: 2, z: 4, core: 2. Of those that a mesh axis runs over, the one named last changes fastest.
Arguments:
- tracer: float32 [2, 100, 16, 1024], P(None, 'gz', None, 'gx'), may hold values from -6 to 6
- east_flow: float32 [100, 16, 1024], P('gz', None, 'gx'), may hold values from -0.35 to 0.35
- north_flow: float32 [100, 16, 1024], P('gz', None, 'gx'), may hold values from -0.35 to 0.35
- vertical_flow: float32 [100, 16, 1024], P('gz', None, 'gx'), may hold values from -0.3 to 0.3
- mixing_lateral: float32 [100, 16, 1024], P('gz', None, 'gx'), may hold values from 0.02 to 0.12
- mixing_vertical: float32 [100, 16, 1024], P('gz', None, 'gx'), may hold values from 0.5 to 500
- sea_mask: int32 [100, 16, 1024], P('gz', None, 'gx'), may hold values 0 or 1
- bottom: int32 [16, 1024], P(None, 'gx'), may hold values from 25 to 100
Outputs:
- updated: float32 [2, 100, 16, 1024], P(None, 'gz', None, 'gx')
The draws below stay inside these ranges and needn't reach their ends.
All inputs are finite; a program needn't handle non-finite values. No bound on the sum of `sea_mask` on one device may be relied on, other than what follows from the above.
Results may differ from the reference program's by a relative error of at most 0.000032.
Values sent between devices are 32-bit elements; how exact they have to be, the bound alone decides.
No kernel may reach another device: no remote copies, remote signals or barrier semaphores. Data moves between devices by JAX's collectives and lax.ppermute only.
A program may use at most 64 MiB of HBM per device.

```python
import math
import jax
import jax.numpy as jnp
from jax import lax

NTR = 2
LEV = 100
SUB = 3
NY = 16
NX = 1024


def place_ends(values, key, least, top_value):
    index_at = [jax.random.randint(jax.random.fold_in(key, axis), (), 0, length) for axis, length in enumerate(values.shape)]
    longest = values.shape.index(max(values.shape))
    neighbour = index_at[:longest] + [(index_at[longest] + 1) % values.shape[longest]] + index_at[longest + 1:]
    return values.at[tuple(index_at)].set(least).at[tuple(neighbour)].set(top_value)


def level_of(rng, shape, shards, low, top_value):
    def one(position, shards_of):
        steps = jax.random.uniform(jax.random.fold_in(jax.random.fold_in(rng, 6), position), (shards_of,), jnp.float32, low / len(shards), top_value / len(shards))
        return jnp.repeat(jnp.exp(steps), shape[position] // shards_of).reshape((-1,) + (1,) * (len(shape) - position - 1))

    level = one(*shards[0])
    for cut in shards[1:]:
        level = level * one(*cut)
    return level


def gaussian(own_key, dims, deviation, most, pieces=(), kind=jnp.bfloat16):
    drawn = jax.random.normal(own_key, dims, jnp.float32) * deviation
    if len(pieces) > 0:
        drawn = level_of(own_key, dims, pieces, -0.22, 0.18) * drawn
    return jnp.clip(drawn, min=-most, max=most).astype(kind)


def setup_inputs(seed: int = 0) -> dict:
    seeds = jax.random.split(jax.random.key(seed), 9)
    tracer = gaussian(seeds[0], (NTR, LEV, NY, NX), 1.0, 6.0, ((1, 4), (3, 8)), jnp.float32)
    east_flow = jnp.clip(jax.random.uniform(seeds[1], (LEV, NY, NX), jnp.float32, -0.35, 0.35) * level_of(seeds[1], (LEV, NY, NX), ((0, 4), (2, 8)), -0.4, 0.0), -0.35, 0.35)
    north_flow = jnp.clip(jax.random.uniform(seeds[2], (LEV, NY, NX), jnp.float32, -0.35, 0.35) * level_of(seeds[2], (LEV, NY, NX), ((0, 4), (2, 8)), -0.4, 0.0), -0.35, 0.35)
    vertical_flow = jnp.clip(jax.random.uniform(seeds[3], (LEV, NY, NX), jnp.float32, -0.3, 0.3) * level_of(seeds[3], (LEV, NY, NX), ((0, 4), (2, 8)), -0.4, 0.0), -0.3, 0.3)
    mixing_lateral = jnp.clip(jnp.exp(math.log(0.12) - 1.7917595 * jax.random.uniform(seeds[4], (LEV, NY, NX), jnp.float32) ** level_of(seeds[4], (LEV, NY, NX), ((0, 4), (2, 8)), -0.2, 0.2)), 0.02, 0.12)
    mixing_vertical = jnp.clip(jnp.exp(math.log(500.0) - 6.9077553 * jax.random.uniform(seeds[5], (LEV, NY, NX), jnp.float32) ** level_of(seeds[5], (LEV, NY, NX), ((0, 4), (2, 8)), -0.2, 0.2)), 0.5, 500.0)
    sea_mask = place_ends((jax.random.randint(seeds[6], (LEV, NY, NX), 0, 32) < 31).astype(jnp.int32), jax.random.fold_in(seeds[6], 1), 0, 1)
    bottom = place_ends(jax.random.randint(seeds[7], (NY, NX), LEV // 4, LEV + 1), jax.random.fold_in(seeds[7], 1), LEV // 4, LEV).astype(jnp.int32)
    return {"tracer": tracer, "east_flow": east_flow, "north_flow": north_flow, "vertical_flow": vertical_flow, "mixing_lateral": mixing_lateral, "mixing_vertical": mixing_vertical, "sea_mask": sea_mask, "bottom": bottom}


def horizontal_step(content, east_speed, diffusion, wet_cells, north_speed):
    west_side = content[..., :-1]
    east_side = content[..., 1:]
    open_faces = wet_cells[..., :-1] * wet_cells[..., 1:]
    flow_east = east_speed[..., :-1]
    flux_east = open_faces * (jnp.maximum(flow_east, 0.0) * west_side + jnp.minimum(flow_east, 0.0) * east_side
                              + 0.5 * (diffusion[..., :-1] + diffusion[..., 1:]) * (west_side - east_side))
    net_east = flux_east[..., 1:] - flux_east[..., :-1]
    interior = content[..., 1:-1]
    wet_inner = wet_cells[..., 1:-1]
    diff_inner = diffusion[..., 1:-1]
    south_side = interior[..., :-1, :]
    north_side = interior[..., 1:, :]
    open_rows = wet_inner[..., :-1, :] * wet_inner[..., 1:, :]
    north_face = north_speed[..., :-1, :]
    flux_north = open_rows * (jnp.maximum(north_face, 0.0) * south_side + jnp.minimum(north_face, 0.0) * north_side
                              + 0.5 * (diff_inner[..., :-1, :] + diff_inner[..., 1:, :]) * (south_side - north_side))
    wall_rows = jnp.zeros_like(flux_north[..., :1, :])
    padded = jnp.concatenate([wall_rows, flux_north, wall_rows], axis=-2)
    net_north = padded[..., 1:, :] - padded[..., :-1, :]
    return interior - wet_inner * (net_east + net_north)


def vertical_step(content, upward, wet_cells):
    upper_cells = content[..., :-1, :, :]
    lower_cells = content[..., 1:, :, :]
    open_faces = wet_cells[:-1] * wet_cells[1:]
    face_speed = upward[:-1]
    flux_up = open_faces * (jnp.maximum(face_speed, 0.0) * lower_cells + jnp.minimum(face_speed, 0.0) * upper_cells)
    return content[..., 1:-1, :, :] + wet_cells[1:-1] * (flux_up[..., 1:, :, :] - flux_up[..., :-1, :, :])


def implicit_mix(content, mixing, wet_cells):
    coupling = mixing[:-1] * wet_cells[:-1] * wet_cells[1:]
    zeroes = jnp.zeros_like(coupling[:1])
    upper_link = jnp.concatenate([zeroes, coupling], axis=0)
    lower_link = jnp.concatenate([coupling, zeroes], axis=0)
    diagonal = 1.0 + upper_link + lower_link
    levels = content.shape[1]
    ratios = []
    values = []
    for level_id in range(levels):
        if level_id == 0:
            divisor = diagonal[0]
            forcing = content[:, 0]
        else:
            divisor = diagonal[level_id] - upper_link[level_id] * ratios[-1]
            forcing = content[:, level_id] + upper_link[level_id] * values[-1]
        ratios.append(lower_link[level_id] / divisor)
        values.append(forcing / divisor)
    solved = [values[-1]]
    for level_id in range(levels - 2, -1, -1):
        solved.append(values[level_id] + ratios[level_id] * solved[-1])
    return jnp.stack(solved[::-1], axis=1)


def pad_levels(array):
    widths = [(0, 0)] * (array.ndim - 3) + [(1, 1), (0, 0), (0, 0)]
    return jnp.pad(array, widths)


def wrapped(array):
    return jnp.concatenate([array[..., -1:], array, array[..., :1]], axis=-1)


def reference(tracer, east_flow, north_flow, vertical_flow, mixing_lateral, mixing_vertical, sea_mask, bottom):
    level_index = lax.broadcasted_iota(jnp.int32, sea_mask.shape, 0)
    wet_cells = sea_mask.astype(jnp.float32) * (level_index < bottom[None]).astype(jnp.float32)
    tracers_now = tracer
    for substep in range(SUB):
        tracers_now = horizontal_step(wrapped(tracers_now), wrapped(east_flow), wrapped(mixing_lateral),
                                      wrapped(wet_cells), north_flow)
    tracers_now = vertical_step(pad_levels(tracers_now), pad_levels(vertical_flow), pad_levels(wet_cells))
    return implicit_mix(tracers_now, mixing_vertical, wet_cells)
```

```python
import functools

import jax
import jax.numpy as jnp
from jax import lax
from jax.experimental import pallas as pl
from jax.experimental.pallas import tpu as pltpu
from jax.sharding import PartitionSpec as P

SUB = 3
SLOT = 3 * SUB
GROUP = SLOT // SUB

VMEM = pl.BlockSpec(memory_space=pltpu.VMEM)


def call(kernel, shapes, flops, *operands):
    outs = [jax.ShapeDtypeStruct(s, jnp.float32) for s in shapes]
    size = sum(o.size * o.dtype.itemsize for o in (*operands, *outs))
    return pl.pallas_call(
        kernel,
        out_shape=outs,
        in_specs=[VMEM] * len(operands),
        out_specs=[VMEM] * len(outs),
        compiler_params=pltpu.CompilerParams(vmem_limit_bytes=24 * 2**20),
        cost_estimate=pl.CostEstimate(flops=flops, bytes_accessed=size, transcendentals=0),
    )(*operands)


def rolled(plane, shift, axis):
    return pltpu.roll(plane, shift % plane.shape[axis], axis)


def lanes_of(plane):
    return lax.broadcasted_iota(jnp.int32, plane.shape, 1)


def wetness(mask_ref, bottom, level, first_level):
    return jnp.where((mask_ref[level] > 0) & (first_level + level < bottom), 1.0, 0.0)


def lateral_coefficients(east, north, mixing, wet):
    rows = east.shape[0]
    open_east = wet * rolled(wet, -1, 1)
    mean_east = 0.5 * (mixing + rolled(mixing, -1, 1))
    row = lax.broadcasted_iota(jnp.int32, wet.shape, 0)
    open_north = jnp.where(row < rows - 1, wet * rolled(wet, -1, 0), 0.0)
    mean_north = 0.5 * (mixing + rolled(mixing, -1, 0))
    return (
        open_east * (jnp.maximum(east, 0.0) + mean_east),
        open_east * (jnp.minimum(east, 0.0) - mean_east),
        open_north * (jnp.maximum(north, 0.0) + mean_north),
        open_north * (jnp.minimum(north, 0.0) - mean_north),
    )


def lateral_substeps(content, coefficients):
    from_here, from_east, from_row, from_north = coefficients
    for _ in range(SUB):
        flux_east = from_here * content + from_east * rolled(content, -1, 1)
        flux_north = from_row * content + from_north * rolled(content, -1, 0)
        content = content - (
            (flux_east - rolled(flux_east, 1, 1)) + (flux_north - rolled(flux_north, 1, 0))
        )
    return content


def slots_of(levels, width):
    per_tile = width // SLOT
    tiles = -(-levels // per_tile)
    return [[(s, t * per_tile + s) for s in range(min(per_tile, levels - t * per_tile))] for t in range(tiles)]


def window_tile(plane_of, slots, offset):
    tile = None
    for slot, level in slots:
        moved = rolled(plane_of(level), SLOT * slot + offset, 1)
        tile = moved if tile is None else jnp.where(lanes_of(moved) >= SLOT * slot, moved, tile)
    return tile


def plane_readers(tracer_ref, east_ref, north_ref, mixing_ref, wet_of):
    tracers = [functools.partial(lambda i, k: tracer_ref[i, k], i) for i in range(tracer_ref.shape[0])]
    return tracers + [lambda k: east_ref[k], lambda k: north_ref[k], lambda k: mixing_ref[k], wet_of]


def pack_kernel(tracer, east, north, mixing, mask, bottom, east_tiles, to_far, to_near):
    levels, _, width = mask.shape
    first_level = lax.axis_index("gz") * levels
    even = lax.axis_index("gx") % 2 == 0
    wet_of = lambda k: wetness(mask, bottom[...], k, first_level)
    readers = plane_readers(tracer, east, north, mixing, wet_of)
    for t, slots in enumerate(slots_of(levels, width)):
        tiles = [window_tile(reader, slots, 2 * SUB) for reader in readers]
        for j, tile in enumerate(tiles):
            east_tiles[j, t] = tile
        for g in range(to_far.shape[0]):
            east_part = west_part = None
            for q in range(GROUP):
                if g * GROUP + q >= len(tiles):
                    break
                tile = tiles[g * GROUP + q]
                e = rolled(tile, SUB * (q - 1), 1)
                w = rolled(tile, SUB * (q - 2), 1)
                if q == 0:
                    east_part, west_part = e, w
                else:
                    inside = lax.rem(lanes_of(tile), SLOT) >= SUB * q
                    east_part = jnp.where(inside, e, east_part)
                    west_part = jnp.where(inside, w, west_part)
            to_far[g, t] = jnp.where(even, west_part, east_part)
            to_near[g, t] = jnp.where(even, east_part, west_part)


def interior_kernel(
    tracer, east, north, vertical, mixing, mixing_vertical, mask, bottom,
    west_tiles, lateral, down, up, from_first, from_last, pivots, ratios, carries, rims,
):
    levels, _, width = mask.shape
    first_level = lax.axis_index("gz") * levels
    wet_of = lambda k: wetness(mask, bottom[...], k, first_level)
    wet_first = wet = wet_of(0)
    couplings = []
    rest = jnp.ones_like(wet)
    for k in range(levels - 1):
        wet_below = wet_of(k + 1)
        both = wet * wet_below
        coupling = mixing_vertical[k] * both
        speed = vertical[k] * both
        down[k] = jnp.maximum(speed, 0.0)
        up[k] = jnp.minimum(speed, 0.0)
        inverse = 1.0 / (rest + coupling)
        pivots[k] = inverse
        ratio = coupling * inverse
        ratios[k] = ratio
        carries[k] = coupling
        rest = 1.0 + ratio * rest
        couplings.append(coupling)
        wet = wet_below
    weight = 1.0 / rest
    pivots[levels - 1] = weight
    from_last[levels - 1] = weight
    last_own = weight
    for k in range(levels - 2, -1, -1):
        weight = ratios[k] * weight
        from_last[k] = weight
    across = weight
    rest = jnp.ones_like(wet)
    upward = []
    for k in range(levels - 2, -1, -1):
        ratio = couplings[k] / (rest + couplings[k])
        upward.append(ratio)
        rest = 1.0 + ratio * rest
    weight = 1.0 / rest
    from_first[0] = weight
    for k in range(levels - 1):
        weight = upward[levels - 2 - k] * weight
        from_first[k + 1] = weight
    link = wet * mixing_vertical[levels - 1]
    speed = wet * vertical[levels - 1]
    scale = 1.0 / (1.0 + link * last_own)
    rims[0] = link * scale
    rims[1] = jnp.maximum(speed, 0.0) * scale
    rims[2] = jnp.minimum(speed, 0.0) * scale
    rims[3] = wet_first * rest
    rims[4] = across
    for k in range(levels):
        coefficients = lateral_coefficients(east[k], north[k], mixing[k], wet_of(k))
        for i in range(tracer.shape[0]):
            lateral[i, k] = lateral_substeps(tracer[i, k], coefficients)
    readers = plane_readers(tracer, east, north, mixing, wet_of)
    for t, slots in enumerate(slots_of(levels, width)):
        for j, reader in enumerate(readers):
            west_tiles[j, t] = window_tile(reader, slots, SUB)


def rim_kernel(
    east_tiles, west_tiles, far, near, lateral, down, up, from_first, from_last, rims,
    forcing, message,
):
    tracers, levels, _, width = lateral.shape
    even = lax.axis_index("gx") % 2 == 0
    edges = []
    for t, slots in enumerate(slots_of(levels, width)):
        lane = lax.rem(lanes_of(bottom_like(lateral)), SLOT)
        from_west = [jnp.where(even, far[g, t], near[g, t]) for g in range(far.shape[0])]
        from_east = [jnp.where(even, near[g, t], far[g, t]) for g in range(far.shape[0])]
        west, east = [], []
        for j in range(east_tiles.shape[0]):
            g, q = divmod(j, GROUP)
            west.append(jnp.where(lane < SUB, rolled(from_west[g], -SUB * q, 1), west_tiles[j, t]))
            east.append(
                jnp.where(lane >= 2 * SUB, rolled(from_east[g], SUB * (2 - q), 1), east_tiles[j, t])
            )
        west_steps = lateral_coefficients(*west[tracers:])
        east_steps = lateral_coefficients(*east[tracers:])
        done = []
        for i in range(tracers):
            west_done = lateral_substeps(west[i], west_steps)
            east_done = lateral_substeps(east[i], east_steps)
            done.append(jnp.where(lane < SUB, rolled(east_done, -SUB, 1), west_done))
        edges.append(done)
    per_tile = width // SLOT
    for i in range(tracers):
        above = flux_above = None
        first_sum = last_sum = None
        for k in range(levels + 1):
            if k < levels:
                t, s = divmod(k, per_tile)
                edge = rolled(edges[t][i], width - SUB - SLOT * s, 1)
                lane = lanes_of(edge)
                here = jnp.where((lane < SUB) | (lane >= width - SUB), edge, lateral[i, k])
            if k == 0:
                first = above = here
                continue
            if k < levels:
                flux = down[k - 1] * here + up[k - 1] * above
                value = above + (flux if k == 1 else flux - flux_above)
                flux_above = flux
            else:
                value = above - flux_above
            forcing[i, k - 1] = value
            a = from_first[k - 1] * value
            b = from_last[k - 1] * value
            first_sum = a if k == 1 else first_sum + a
            last_sum = b if k == 1 else last_sum + b
            above = here
        message[i] = rims[0] * last_sum - rims[2] * above
        message[tracers + 2 + i] = rims[3] * first_sum
        message[2 * tracers + 2 + i] = rims[3] * first
    message[tracers] = rims[0]
    message[tracers + 1] = rims[1]
    message[3 * tracers + 2] = rims[3]
    message[3 * tracers + 3] = rims[4]


def bottom_like(ref):
    return jnp.zeros(ref.shape[-2:], jnp.float32)


def block_kernel(forcing, pivots, ratios, carries, solved):
    tracers, levels = forcing.shape[:2]
    for i in range(tracers):
        value = forcing[i, 0] * pivots[0]
        values = [value]
        for k in range(1, levels):
            value = (forcing[i, k] + carries[k - 1] * value) * pivots[k]
            values.append(value)
        solved[i, levels - 1] = value
        for k in range(levels - 2, -1, -1):
            value = values[k] + ratios[k] * value
            solved[i, k] = value


def interface(upper, lower, tracers):
    heads, alpha, beta = upper[:tracers], upper[tracers], upper[tracers + 1]
    sums, rims, admit = lower[:tracers], lower[tracers : 2 * tracers], lower[2 * tracers]
    inverse = jnp.where(admit > 0.0, 1.0 / (admit + alpha), 0.0)
    flux = [(alpha * s + beta * r - admit * h) * inverse for s, r, h in zip(sums, rims, heads)]
    return flux, admit * alpha * inverse


def pair_kernel(own, other, merged, kept):
    tracers = kept.shape[0] - 1
    z = lax.axis_index("gz")
    lower_here = z % 2 == 1
    lower_pair = z >= 2
    upper, lower = [], []
    count = own.shape[0]
    for j in range(count):
        upper.append(jnp.where(lower_here, other[j], own[j]))
        lower.append(jnp.where(lower_here, own[j], other[j]))
    n = tracers + 2
    flux, gain = interface(upper[:n], lower[n:-1], tracers)
    across = jnp.where(lower_pair, upper[-1], lower[-1])
    gain = gain * across
    for i in range(tracers):
        kept[i] = flux[i]
    kept[tracers] = gain
    factor = across * jnp.where(lower_pair, upper[-2], lower[tracers])
    scale = 1.0 / (1.0 - factor * gain)
    for i in range(tracers):
        head = jnp.where(lower_pair, upper[n + i] + factor * flux[i], lower[i] - factor * flux[i])
        merged[i] = head * scale
    for i in range(tracers + 1):
        merged[tracers + i] = scale * (
            jnp.where(lower_pair, upper[n + tracers + i], lower[tracers + i] if i < 2 else 0.0)
        )


def final_kernel(own, other, kept, solved, from_first, from_last, out):
    tracers, levels = solved.shape[:2]
    z = lax.axis_index("gz")
    lower_pair = z >= 2
    upper = [jnp.where(lower_pair, other[j], own[j]) for j in range(own.shape[0])]
    lower = [jnp.where(lower_pair, own[j], other[j]) for j in range(own.shape[0])]
    middle, _ = interface(upper[: tracers + 2], lower, tracers)
    for i in range(tracers):
        near = kept[i] + kept[tracers] * middle[i]
        top = jnp.where(z == 0, 0.0, jnp.where(z == 2, middle[i], near))
        low = jnp.where(z == 3, 0.0, jnp.where(z == 1, middle[i], near))
        for k in range(levels):
            out[i, k] = solved[i, k] - top * from_first[k] + low * from_last[k]


def local(
    tracer, east_flow, north_flow, vertical_flow, mixing_lateral, mixing_vertical, sea_mask, bottom
):
    tracers, levels, rows, width = tracer.shape
    arrays = tracers + 4
    tiles = len(slots_of(levels, width))
    groups = -(-arrays // GROUP)
    plane = (rows, width)
    block = (levels, rows, width)
    ring = lax.axis_size("gx")
    cells = levels * rows * width
    near_pairs = [(i, i ^ 1) for i in range(ring)]
    far_pairs = [(i, (i + 1) % ring if i % 2 else (i - 1) % ring) for i in range(ring)]

    east_tiles, to_far, to_near = call(
        pack_kernel,
        [(arrays, tiles) + plane, (groups, tiles) + plane, (groups, tiles) + plane],
        10 * cells,
        tracer, east_flow, north_flow, mixing_lateral, sea_mask, bottom,
    )
    far = lax.ppermute(to_far, "gx", far_pairs)
    near = lax.ppermute(to_near, "gx", near_pairs)
    west_tiles, lateral, down, up, from_first, from_last, pivots, ratios, carries, rims = call(
        interior_kernel,
        [(arrays, tiles) + plane, tracer.shape] + [block] * 7 + [(5,) + plane],
        150 * cells,
        tracer, east_flow, north_flow, vertical_flow, mixing_lateral, mixing_vertical, sea_mask, bottom,
    )
    forcing, message = call(
        rim_kernel,
        [tracer.shape, (3 * tracers + 4,) + plane],
        40 * cells,
        east_tiles, west_tiles, far, near, lateral, down, up, from_first, from_last, rims,
    )
    other = lax.ppermute(message, "gz", [(i, i ^ 1) for i in range(4)])
    (solved,) = call(block_kernel, [tracer.shape], 30 * cells, forcing, pivots, ratios, carries)
    merged, kept = call(
        pair_kernel, [(2 * tracers + 1,) + plane, (tracers + 1,) + plane], cells, message, other
    )
    beyond = lax.ppermute(merged, "gz", [(i, i ^ 2) for i in range(4)])
    (result,) = call(
        final_kernel, [tracer.shape], 10 * cells, merged, beyond, kept, solved, from_first, from_last
    )
    return result


def solution(mesh):
    assert mesh.shape["gz"] == 4 and mesh.shape["gx"] % 2 == 0
    return jax.shard_map(
        local,
        mesh=mesh,
        in_specs=(
            P(None, "gz", None, "gx"),
            P("gz", None, "gx"),
            P("gz", None, "gx"),
            P("gz", None, "gx"),
            P("gz", None, "gx"),
            P("gz", None, "gx"),
            P("gz", None, "gx"),
            P(None, "gx"),
        ),
        out_specs=P(None, "gz", None, "gx"),
        check_vma=False,
    )
```

```python
import jax
import jax.numpy as jnp
from jax import lax
from jax.experimental import pallas as pl
from jax.experimental.pallas import tpu as pltpu
from jax.sharding import PartitionSpec as P

SUB = 3
SLOT = 3 * SUB
GROUP = SLOT // SUB

VMEM = pl.BlockSpec(memory_space=pltpu.VMEM)
HBM = pl.BlockSpec(memory_space=pltpu.HBM)


def call(kernel, shapes, flops, *operands, in_specs=None, out_specs=None, scratch=()):
    outs = [jax.ShapeDtypeStruct(s, jnp.float32) for s in shapes]
    if in_specs is not None:
        operands = [pltpu.with_memory_space_constraint(x, pltpu.HBM) if p is HBM else x for x, p in zip(operands, in_specs)]
    size = sum(o.size * o.dtype.itemsize for o in (*operands, *outs))
    return pl.pallas_call(
        kernel,
        out_shape=outs,
        in_specs=in_specs or [VMEM] * len(operands),
        out_specs=out_specs or [VMEM] * len(outs),
        scratch_shapes=list(scratch),
        compiler_params=pltpu.CompilerParams(vmem_limit_bytes=24 * 2**20),
        cost_estimate=pl.CostEstimate(flops=flops, bytes_accessed=size, transcendentals=0),
    )(*operands)


def rolled(plane, shift, axis):
    return pltpu.roll(plane, shift % plane.shape[axis], axis)


def lanes_of(plane):
    return lax.broadcasted_iota(jnp.int32, plane.shape, 1)


def lateral_coefficients(east, north, mixing, wet):
    rows = east.shape[0]
    open_east = wet * rolled(wet, -1, 1)
    mean_east = 0.5 * (mixing + rolled(mixing, -1, 1))
    row = lax.broadcasted_iota(jnp.int32, wet.shape, 0)
    open_north = jnp.where(row < rows - 1, wet * rolled(wet, -1, 0), 0.0)
    mean_north = 0.5 * (mixing + rolled(mixing, -1, 0))
    return (
        open_east * (jnp.maximum(east, 0.0) + mean_east),
        open_east * (jnp.minimum(east, 0.0) - mean_east),
        open_north * (jnp.maximum(north, 0.0) + mean_north),
        open_north * (jnp.minimum(north, 0.0) - mean_north),
    )


def lateral_substeps(planes, coefficients):
    for _ in range(SUB):
        east = {q: rolled(c, -1, 1) for q, c in planes.items()}
        flux_east = {q: coefficients[q[1]][0] * c + coefficients[q[1]][1] * east[q] for q, c in planes.items()}
        flux_west = {q: rolled(f, 1, 1) for q, f in flux_east.items()}
        flux_north = {
            q: coefficients[q[1]][2] * c + coefficients[q[1]][3] * rolled(c, -1, 0) for q, c in planes.items()
        }
        planes = {
            q: c - ((flux_east[q] - flux_west[q]) + (flux_north[q] - rolled(flux_north[q], 1, 0)))
            for q, c in planes.items()
        }
    return planes


def stencil(east, north, mixing, wet):
    rows = east.shape[0]
    wet_west, mixing_west, east_west = (rolled(x, 1, 1) for x in (wet, mixing, east))
    open_east = wet * rolled(wet, -1, 1)
    mean_east = 0.5 * (mixing + rolled(mixing, -1, 1))
    open_west = wet * wet_west
    mean_west = 0.5 * (mixing + mixing_west)
    row = lax.broadcasted_iota(jnp.int32, wet.shape, 0)
    open_north = jnp.where(row < rows - 1, wet * rolled(wet, -1, 0), 0.0)
    mean_north = 0.5 * (mixing + rolled(mixing, -1, 0))
    east_in = open_east * (mean_east - jnp.minimum(east, 0.0))
    east_out = open_east * (mean_east + jnp.maximum(east, 0.0))
    west_in = open_west * (mean_west + jnp.maximum(east_west, 0.0))
    west_out = open_west * (mean_west - jnp.minimum(east_west, 0.0))
    north_in = open_north * (mean_north - jnp.minimum(north, 0.0))
    north_out = open_north * (mean_north + jnp.maximum(north, 0.0))
    south_in = rolled(north_out, 1, 0)
    south_out = rolled(north_in, 1, 0)
    here = 1.0 - ((east_out + west_out) + (north_out + south_out))
    return here, east_in, west_in, north_in, south_in


def stencil_substeps(planes, weights):
    for _ in range(SUB):
        sides = {q: (rolled(c, -1, 1), rolled(c, 1, 1), rolled(c, -1, 0), rolled(c, 1, 0)) for q, c in planes.items()}
        planes = {
            q: (weights[q[1]][0] * c + weights[q[1]][3] * sides[q][2] + weights[q[1]][4] * sides[q][3])
            + (weights[q[1]][1] * sides[q][0] + weights[q[1]][2] * sides[q][1])
            for q, c in planes.items()
        }
    return planes


def slots_of(levels, width):
    per_tile = width // SLOT
    tiles = -(-levels // per_tile)
    return [[(s, t * per_tile + s) for s in range(min(per_tile, levels - t * per_tile))] for t in range(tiles)]


def window_tiles(plane_of, slots):
    moved = [(slot, rolled(plane_of(level), SLOT * slot + SUB, 1)) for slot, level in slots]
    lane = lanes_of(moved[0][1])
    tiles = []
    for ahead in (0, SUB):
        parts = moved
        while len(parts) > 1:
            pairs = [parts[n : n + 2] for n in range(0, len(parts), 2)]
            parts = [
                p[0] if len(p) == 1 else (p[0][0], jnp.where(lane >= SLOT * p[1][0] - ahead, p[1][1], p[0][1]))
                for p in pairs
            ]
        tiles.append(parts[0][1])
    return tiles[0], jnp.where(lane >= lane.shape[1] - SUB, moved[0][1], tiles[1])


def pack_group(tiles, first_columns):
    lane = lax.rem(lanes_of(tiles[0]), SLOT)
    packed = None
    for q, tile in enumerate(tiles):
        moved = jnp.where(first_columns, rolled(tile, SUB * (q - 1), 1), rolled(tile, SUB * q, 1))
        packed = moved if q == 0 else jnp.where(lane >= SUB * q, moved, packed)
    return packed


def pack_kernel(
    tracer_in, mixing_in, east_in, north_in, mask_in, bottom_in, vertical_in, mixing_vertical_in,
    tracer, mixing, east, north, wet, vertical, mixing_vertical, west_tiles, east_tiles, to_far, mask, bottom, sems,
):
    levels, _, width = mask.shape
    tracers = tracer.shape[0]
    pairs = [(bottom_in, bottom), (mask_in, mask), (mixing_in, mixing), (east_in, east), (north_in, north)]
    pairs += [(tracer_in.at[i], tracer.at[i]) for i in range(tracers)]
    pairs += [(vertical_in, vertical), (mixing_vertical_in, mixing_vertical)]
    copies = [pltpu.make_async_copy(source, target, sems.at[n]) for n, (source, target) in enumerate(pairs)]
    for copy in copies:
        copy.start()
    slots = slots_of(levels, width)
    even = lax.axis_index("gx") % 2 == 0
    for copy in copies[:4]:
        copy.wait()
    floor = bottom[...] - lax.axis_index("gz") * levels
    signed = []
    for k in range(levels):
        is_wet = (mask[k] > 0) & (k < floor)
        wet[k] = jnp.where(is_wet, 1.0, 0.0)
        signed.append(jnp.where(is_wet, mixing[k], -mixing[k]))
    found = {}

    def find(j, t, pair):
        found[j, t] = pair[0]
        west_tiles[j, t], east_tiles[j, t] = pair

    for t, part in enumerate(slots):
        both = window_tiles(lambda k: signed[k], part)
        find(tracers, t, [jnp.abs(b) for b in both])
        find(tracers + 1, t, [jnp.where(b > 0.0, 1.0, 0.0) for b in both])
        find(tracers + 2, t, window_tiles(lambda k: east[k], part))
    for copy in copies[4:-2]:
        copy.wait()
    for t, part in enumerate(slots):
        for i in range(tracers):
            find(i, t, window_tiles(lambda k: tracer[i, k], part))
        find(tracers + 3, t, window_tiles(lambda k: north[k], part))
    for t in range(len(slots)):
        for g in range(to_far.shape[0]):
            to_far[g, t] = pack_group([found[g * GROUP + q, t] for q in range(GROUP)], even)
    for copy in copies[-2:]:
        copy.wait()


def side_kernel(
    wet, vertical, mixing_vertical, west_tiles,
    to_near, down, up, from_first, from_last, pivots, ratios, couplings, weights, rims,
):
    odd = lax.axis_index("gx") % 2 == 1
    for g, t in [(g, t) for g in range(to_near.shape[0]) for t in range(to_near.shape[1])]:
        to_near[g, t] = pack_group([west_tiles[g * GROUP + q, t] for q in range(GROUP)], odd)
    vertical_statics(
        wet, vertical, mixing_vertical, down, up, from_first, from_last, pivots, ratios, couplings, weights, rims
    )


def interior_kernel(tracer, mixing, east, north, wet, weights, lateral, sums):
    levels = wet.shape[0]
    tracers = tracer.shape[0]
    coefficients = {k: lateral_coefficients(east[k], north[k], mixing[k], wet[k]) for k in range(levels)}
    planes = {(i, k): tracer[i, k] for k in range(levels) for i in range(tracers)}
    planes = lateral_substeps(planes, coefficients)
    for i, k in planes:
        lateral[i, k] = planes[i, k]
    for i in range(tracers):
        for n in range(2):
            sums[n * tracers + i] = total([weights[n, k] * planes[i, k] for k in range(levels)])


def vertical_statics(
    wet_ref, vertical, mixing_vertical, down, up, from_first, from_last, pivots, ratios, couplings, weights, rims
):
    levels = wet_ref.shape[0]
    wet = [wet_ref[k] for k in range(levels)]
    both = [wet[k] * wet[k + 1] for k in range(levels - 1)]
    speeds = [vertical[k] * both[k] for k in range(levels - 1)]
    links = [mixing_vertical[k] * both[k] for k in range(levels - 1)]
    one = jnp.ones_like(wet[0])
    top_p = top_q = low_p = low_q = one
    pivot, ratio, upward = [None] * levels, [None] * levels, [None] * levels
    for k in range(levels - 1):
        next_q = top_p + links[k] * top_q
        next_p = next_q + links[k] * top_p
        inverse = 1.0 / next_q
        pivot[k] = top_q * inverse
        ratio[k] = links[k] * pivot[k]
        top_p, top_q = next_p, next_q
        m = levels - 2 - k
        next_q = low_p + links[m] * low_q
        next_p = next_q + links[m] * low_p
        low_inverse = 1.0 / next_q
        upward[m] = links[m] * low_q * low_inverse
        low_p, low_q = next_p, next_q
        if k % 6 == 5:
            top_p, top_q = top_p * inverse, one
            low_p, low_q = low_p * low_inverse, one
    last, first = [None] * levels, [None] * levels
    last[-1] = pivot[-1] = top_q / top_p
    first[0] = low_q / low_p
    for k in range(levels - 1):
        m = levels - 2 - k
        last[m] = ratio[m] * last[m + 1]
        first[k + 1] = upward[k] * first[k]
    link = wet[-1] * mixing_vertical[levels - 1]
    speed = wet[-1] * vertical[levels - 1]
    scale = 1.0 / (1.0 + link * last[-1])
    rim = [link * scale, jnp.maximum(speed, 0.0) * scale, jnp.minimum(speed, 0.0) * scale]
    rim += [wet[0] * low_p / low_q, last[0]]
    for k in range(levels):
        pivots[k], from_first[k], from_last[k] = pivot[k], first[k], last[k]
    for k in range(levels - 1):
        ratios[k], couplings[k] = ratio[k], links[k]
        down[k], up[k] = jnp.maximum(speeds[k], 0.0), jnp.minimum(speeds[k], 0.0)
    for n, column in enumerate((first, last)):
        for k in range(levels):
            weight = column[k]
            if k < levels - 1:
                weight = weight + jnp.minimum(speeds[k], 0.0) * (column[k] - column[k + 1])
            if k > 0:
                weight = weight + jnp.maximum(speeds[k - 1], 0.0) * (column[k - 1] - column[k])
            weights[n, k] = weight
    for n, value in enumerate(rim):
        rims[n] = value


def rim_kernel(west_tiles, east_tiles, far, near, lateral, weights, sums, rims, edges, message):
    tracers, levels, _, width = lateral.shape
    even = lax.axis_index("gx") % 2 == 0
    slots = slots_of(levels, width)
    arrays, tiles = east_tiles.shape[:2]
    lanes = lanes_of(rims[0])
    lane = lax.rem(lanes, SLOT)
    windows = {}
    for t in range(tiles):
        from_west = [jnp.where(even, far[g, t], near[g, t]) for g in range(far.shape[0])]
        from_east = [jnp.where(even, near[g, t], far[g, t]) for g in range(far.shape[0])]
        for j in range(arrays):
            g, q = divmod(j, GROUP)
            windows[j, t, 0] = jnp.where(lane < SUB, rolled(from_west[g], -SUB * q, 1), west_tiles[j, t])
            windows[j, t, 1] = jnp.where(
                (lane >= SUB) & (lane < 2 * SUB), rolled(from_east[g], SUB * (1 - q), 1), east_tiles[j, t]
            )
    places = [(t, side) for t in range(tiles) for side in range(2)]
    stencils = {p: stencil(*(windows[(tracers + j,) + p] for j in (2, 3, 0, 1))) for p in places}
    done = stencil_substeps({(i, p): windows[(i,) + p] for p in places for i in range(tracers)}, stencils)
    edge = {
        (i, t): jnp.where(lane < SUB, done[i, (t, 1)], done[i, (t, 0)]) for i in range(tracers) for t in range(tiles)
    }
    at_rim = rim_lanes(lanes)
    placed = {(i, k): edge_at(edge[i, t], s) for t in range(tiles) for s, k in slots[t] for i in range(tracers)}
    for i in range(tracers):
        solved = [
            jnp.where(at_rim, total([weights[n, k] * placed[i, k] for k in range(levels)]), sums[n * tracers + i])
            for n in range(2)
        ]
        first = jnp.where(at_rim, placed[i, 0], lateral[i, 0])
        last = jnp.where(at_rim, placed[i, levels - 1], lateral[i, levels - 1])
        message[i] = rims[0] * solved[1] - rims[2] * last
        message[tracers + 2 + i] = rims[3] * solved[0]
        message[2 * tracers + 2 + i] = rims[3] * first
    message[tracers] = rims[0]
    message[tracers + 1] = rims[1]
    message[3 * tracers + 2] = rims[3]
    message[3 * tracers + 3] = rims[4]
    for i, t in edge:
        edges[i, t] = edge[i, t]


def rim_lanes(lanes):
    return (lanes < SUB) | (lanes >= lanes.shape[1] - SUB)


def edge_at(tile, slot):
    return rolled(tile, -SUB - SLOT * slot, 1)


def total(terms):
    while len(terms) > 1:
        terms = [sum(terms[n : n + 2][1:], terms[n]) for n in range(0, len(terms), 2)]
    return terms[0]


def block_kernel(lateral, edges, down, up, pivots, ratios, couplings, from_first, from_last, kept, base, gain):
    tracers, levels, _, width = lateral.shape
    slots = slots_of(levels, width)
    at_rim = rim_lanes(lanes_of(kept[0]))
    here = {
        (i, k): jnp.where(at_rim, edge_at(edges[i, t], s), lateral[i, k])
        for t in range(len(slots))
        for s, k in slots[t]
        for i in range(tracers)
    }
    values = {}
    for i in range(tracers):
        flux = [down[k] * here[i, k + 1] + up[k] * here[i, k] for k in range(levels - 1)]
        for k in range(levels):
            values[i, k] = here[i, k] if k == levels - 1 else here[i, k] + flux[k]
            if k > 0:
                values[i, k] = values[i, k] - flux[k - 1]
    for i in range(tracers):
        values[i, 0] = values[i, 0] * pivots[0]
    for k in range(1, levels):
        for i in range(tracers):
            values[i, k] = (values[i, k] + couplings[k - 1] * values[i, k - 1]) * pivots[k]
    for k in range(levels - 2, -1, -1):
        for i in range(tracers):
            values[i, k] = values[i, k] + ratios[k] * values[i, k + 1]
    z = lax.axis_index("gz")
    pair = [kept[i] for i in range(tracers)] + [kept[tracers]]
    top = [jnp.where((z == 1) | (z == 3), p, 0.0) for p in pair]
    low = [jnp.where((z == 0) | (z == 2), p, 0.0) for p in pair]
    top_gain = jnp.where(z == 2, 1.0, top[tracers])
    low_gain = jnp.where(z == 1, 1.0, low[tracers])
    for k in range(levels):
        gain[k] = low_gain * from_last[k] - top_gain * from_first[k]
        for i in range(tracers):
            base[i, k] = values[i, k] - top[i] * from_first[k] + low[i] * from_last[k]


def interface(upper, lower, tracers):
    heads, alpha, beta = upper[:tracers], upper[tracers], upper[tracers + 1]
    sums, rims, admit = lower[:tracers], lower[tracers : 2 * tracers], lower[2 * tracers]
    inverse = jnp.where(admit > 0.0, 1.0 / (admit + alpha), 0.0)
    flux = [(alpha * s + beta * r - admit * h) * inverse for s, r, h in zip(sums, rims, heads)]
    return flux, admit * alpha * inverse


def pair_kernel(own, other, merged, kept):
    tracers = kept.shape[0] - 1
    z = lax.axis_index("gz")
    lower_here = z % 2 == 1
    lower_pair = z >= 2
    upper, lower = [], []
    count = own.shape[0]
    for j in range(count):
        upper.append(jnp.where(lower_here, other[j], own[j]))
        lower.append(jnp.where(lower_here, own[j], other[j]))
    n = tracers + 2
    flux, gain = interface(upper[:n], lower[n:-1], tracers)
    across = jnp.where(lower_pair, upper[-1], lower[-1])
    gain = gain * across
    for i in range(tracers):
        kept[i] = flux[i]
    kept[tracers] = gain
    factor = across * jnp.where(lower_pair, upper[-2], lower[tracers])
    scale = 1.0 / (1.0 - factor * gain)
    for i in range(tracers):
        head = jnp.where(lower_pair, upper[n + i] + factor * flux[i], lower[i] - factor * flux[i])
        merged[i] = head * scale
    for i in range(tracers + 1):
        merged[tracers + i] = scale * (
            jnp.where(lower_pair, upper[n + tracers + i], lower[tracers + i] if i < 2 else 0.0)
        )


def final_kernel(own, other, base, gain, out, staged, sems):
    tracers, levels = base.shape[:2]
    lower_pair = lax.axis_index("gz") >= 2
    upper = [jnp.where(lower_pair, other[j], own[j]) for j in range(own.shape[0])]
    lower = [jnp.where(lower_pair, own[j], other[j]) for j in range(own.shape[0])]
    middle, _ = interface(upper[: tracers + 2], lower, tracers)
    copies = []
    for i in range(tracers):
        for k in range(levels):
            staged[i, k] = base[i, k] + middle[i] * gain[k]
        copies.append(pltpu.make_async_copy(staged.at[i], out.at[i], sems.at[i]))
        copies[i].start()
    for copy in copies:
        copy.wait()


def local(
    tracer, east_flow, north_flow, vertical_flow, mixing_lateral, mixing_vertical, sea_mask, bottom
):
    tracers, levels, rows, width = tracer.shape
    arrays = tracers + 4
    tiles = len(slots_of(levels, width))
    assert arrays == 2 * GROUP
    plane = (rows, width)
    block = (levels, rows, width)
    ring = lax.axis_size("gx")
    cells = levels * rows * width
    near_pairs = [(i, i ^ 1) for i in range(ring)]
    far_pairs = [(i, (i + 1) % ring if i % 2 else (i - 1) % ring) for i in range(ring)]

    tracer_here, mixing, east, north, wet, vertical, mixing_down, west_tiles, east_tiles, to_far = call(
        pack_kernel,
        [tracer.shape] + [block] * 6 + [(arrays, tiles) + plane] * 2 + [(2, tiles) + plane],
        20 * cells,
        tracer, mixing_lateral, east_flow, north_flow, sea_mask, bottom, vertical_flow, mixing_vertical,
        in_specs=[HBM] * 8,
        scratch=[
            pltpu.VMEM(block, jnp.int32),
            pltpu.VMEM(plane, jnp.int32),
            pltpu.SemaphoreType.DMA((tracers + 7,)),
        ],
    )
    far = lax.ppermute(to_far, "gx", far_pairs)
    to_near, down, up, from_first, from_last, pivots, ratios, couplings, weights, rims = call(
        side_kernel,
        [(2, tiles) + plane] + [block] * 7 + [(2,) + block, (5,) + plane],
        50 * cells,
        wet, vertical, mixing_down, west_tiles,
    )
    near = lax.ppermute(to_near, "gx", near_pairs)
    lateral, sums = call(
        interior_kernel,
        [tracer.shape, (2 * tracers,) + plane],
        100 * cells,
        tracer_here, mixing, east, north, wet, weights,
    )
    edges, message = call(
        rim_kernel,
        [(tracers, tiles) + plane, (3 * tracers + 4,) + plane],
        20 * cells,
        west_tiles, east_tiles, far, near, lateral, weights, sums, rims,
    )
    other = lax.ppermute(message, "gz", [(i, i ^ 1) for i in range(4)])
    merged, kept = call(
        pair_kernel, [(2 * tracers + 1,) + plane, (tracers + 1,) + plane], cells, message, other
    )
    beyond = lax.ppermute(merged, "gz", [(i, i ^ 2) for i in range(4)])
    base, gain = call(
        block_kernel,
        [tracer.shape, block],
        40 * cells,
        lateral, edges, down, up, pivots, ratios, couplings, from_first, from_last, kept,
    )
    (result,) = call(
        final_kernel, [tracer.shape], 10 * cells, merged, beyond, base, gain,
        out_specs=[HBM],
        scratch=[pltpu.VMEM(tracer.shape, jnp.float32), pltpu.SemaphoreType.DMA((tracers,))],
    )
    return result


def solution(mesh):
    assert mesh.shape["gz"] == 4 and mesh.shape["gx"] % 2 == 0
    return jax.shard_map(
        local,
        mesh=mesh,
        in_specs=(
            P(None, "gz", None, "gx"),
            P("gz", None, "gx"),
            P("gz", None, "gx"),
            P("gz", None, "gx"),
            P("gz", None, "gx"),
            P("gz", None, "gx"),
            P("gz", None, "gx"),
            P(None, "gx"),
        ),
        out_specs=P(None, "gz", None, "gx"),
        check_vma=False,
    )
```

```python
import jax
import jax.numpy as jnp
from jax import lax
from jax.experimental import pallas as pl
from jax.experimental.pallas import tpu as pltpu
from jax.sharding import PartitionSpec as P

SUB = 3
SLOT = 3 * SUB
GROUP = SLOT // SUB

VMEM = pl.BlockSpec(memory_space=pltpu.VMEM)
HBM = pl.BlockSpec(memory_space=pltpu.HBM)


def call(kernel, shapes, flops, *operands, in_specs=None, out_specs=None, scratch=()):
    outs = [jax.ShapeDtypeStruct(s, jnp.float32) for s in shapes]
    if in_specs is not None:
        operands = [pltpu.with_memory_space_constraint(x, pltpu.HBM) if p is HBM else x for x, p in zip(operands, in_specs)]
    size = sum(o.size * o.dtype.itemsize for o in (*operands, *outs))
    return pl.pallas_call(
        kernel,
        out_shape=outs,
        in_specs=in_specs or [VMEM] * len(operands),
        out_specs=out_specs or [VMEM] * len(outs),
        scratch_shapes=list(scratch),
        compiler_params=pltpu.CompilerParams(vmem_limit_bytes=24 * 2**20),
        cost_estimate=pl.CostEstimate(flops=flops, bytes_accessed=size, transcendentals=0),
    )(*operands)


def rolled(plane, shift, axis):
    shift = shift % plane.shape[axis]
    return pltpu.roll(plane, shift, axis) if shift else plane


def lanes_of(plane):
    return lax.broadcasted_iota(jnp.int32, plane.shape, 1)


def places_of(plane, behind):
    factor = -(-512 // SLOT)
    assert all(n * factor >> 9 == n // SLOT for n in range(plane.shape[1] + SLOT))
    lane = lanes_of(plane) + jnp.where(behind, SLOT - SUB, 0)
    return lane - SLOT * ((lane * factor) >> 9)


def lateral_coefficients(east, north, mixing, wet):
    rows = east.shape[0]
    open_east = wet * rolled(wet, -1, 1)
    mean_east = 0.5 * (mixing + rolled(mixing, -1, 1))
    row = lax.broadcasted_iota(jnp.int32, wet.shape, 0)
    open_north = jnp.where(row < rows - 1, wet * rolled(wet, -1, 0), 0.0)
    mean_north = 0.5 * (mixing + rolled(mixing, -1, 0))
    return (
        open_east * (jnp.maximum(east, 0.0) + mean_east),
        open_east * (jnp.minimum(east, 0.0) - mean_east),
        open_north * (jnp.maximum(north, 0.0) + mean_north),
        open_north * (jnp.minimum(north, 0.0) - mean_north),
    )


def lateral_substeps(planes, coefficients):
    for _ in range(SUB):
        east = {q: rolled(c, -1, 1) for q, c in planes.items()}
        flux_east = {q: coefficients[q[1]][0] * c + coefficients[q[1]][1] * east[q] for q, c in planes.items()}
        flux_west = {q: rolled(f, 1, 1) for q, f in flux_east.items()}
        flux_north = {
            q: coefficients[q[1]][2] * c + coefficients[q[1]][3] * rolled(c, -1, 0) for q, c in planes.items()
        }
        planes = {
            q: c - ((flux_east[q] - flux_west[q]) + (flux_north[q] - rolled(flux_north[q], 1, 0)))
            for q, c in planes.items()
        }
    return planes


def stencil(east, north, mixing, wet):
    rows = east.shape[0]
    wet_west, mixing_west, east_west = (rolled(x, 1, 1) for x in (wet, mixing, east))
    open_east = wet * rolled(wet, -1, 1)
    mean_east = 0.5 * (mixing + rolled(mixing, -1, 1))
    open_west = wet * wet_west
    mean_west = 0.5 * (mixing + mixing_west)
    row = lax.broadcasted_iota(jnp.int32, wet.shape, 0)
    open_north = jnp.where(row < rows - 1, wet * rolled(wet, -1, 0), 0.0)
    mean_north = 0.5 * (mixing + rolled(mixing, -1, 0))
    east_in = open_east * (mean_east - jnp.minimum(east, 0.0))
    east_out = open_east * (mean_east + jnp.maximum(east, 0.0))
    west_in = open_west * (mean_west + jnp.maximum(east_west, 0.0))
    west_out = open_west * (mean_west - jnp.minimum(east_west, 0.0))
    north_in = open_north * (mean_north - jnp.minimum(north, 0.0))
    north_out = open_north * (mean_north + jnp.maximum(north, 0.0))
    south_in = rolled(north_out, 1, 0)
    south_out = rolled(north_in, 1, 0)
    here = 1.0 - ((east_out + west_out) + (north_out + south_out))
    return here, east_in, west_in, north_in, south_in


def stencil_substeps(planes, weights):
    for _ in range(SUB):
        sides = {q: (rolled(c, -1, 1), rolled(c, 1, 1), rolled(c, -1, 0), rolled(c, 1, 0)) for q, c in planes.items()}
        planes = {
            q: (weights[q[1]][0] * c + weights[q[1]][3] * sides[q][2] + weights[q[1]][4] * sides[q][3])
            + (weights[q[1]][1] * sides[q][0] + weights[q[1]][2] * sides[q][1])
            for q, c in planes.items()
        }
    return planes


def slots_of(levels, width):
    per_tile = width // SLOT
    tiles = -(-levels // per_tile)
    return [[(s, t * per_tile + s) for s in range(min(per_tile, levels - t * per_tile))] for t in range(tiles)]


def window_tiles(plane_of, slots):
    moved = [(slot, rolled(plane_of(level), SLOT * slot + SUB, 1)) for slot, level in slots]
    lane = lanes_of(moved[0][1])
    tiles = []
    for ahead in (0, SUB):
        parts = moved
        while len(parts) > 1:
            pairs = [parts[n : n + 2] for n in range(0, len(parts), 2)]
            parts = [
                p[0] if len(p) == 1 else (p[0][0], jnp.where(lane >= SLOT * p[1][0] - ahead, p[1][1], p[0][1]))
                for p in pairs
            ]
        tiles.append(parts[0][1])
    return tiles[0], jnp.where(lane >= lane.shape[1] - SUB, moved[0][1], tiles[1])


def pack_group(tiles, first_columns):
    place = places_of(tiles[0], first_columns)
    packed = tiles[0]
    for q, tile in enumerate(tiles[1:], 1):
        packed = jnp.where(place >= SUB * q, rolled(tile, SUB * q, 1), packed)
    return packed


def window_results(own, received, behind, tracers):
    theirs = places_of(own[0, 0], behind) < SUB
    windows = {}
    for j, t in own:
        g, q = divmod(j, GROUP)
        windows[j, t] = jnp.where(theirs, rolled(received[g, t], -SUB * q, 1), own[j, t])
    stencils = {t: stencil(*(windows[tracers + j, t] for j in (2, 3, 0, 1))) for j, t in own if j == 0}
    return stencil_substeps({(j, t): windows[j, t] for j, t in own if j < tracers}, stencils)


def pack_kernel(
    tracer_in, mixing_in, east_in, north_in, mask_in, bottom_in, vertical_in, mixing_vertical_in,
    tracer, mixing, east, north, wet, vertical, mixing_vertical, west_tiles, east_tiles, to_far, to_near, mask, bottom, sems,
):
    levels, _, width = mask.shape
    tracers = tracer.shape[0]
    pairs = [(tracer_in.at[i], tracer.at[i]) for i in range(tracers)]
    pairs += [(east_in, east), (bottom_in, bottom), (mask_in, mask), (north_in, north), (mixing_in, mixing)]
    pairs += [(vertical_in, vertical), (mixing_vertical_in, mixing_vertical)]
    copies = [pltpu.make_async_copy(source, target, sems.at[n]) for n, (source, target) in enumerate(pairs)]
    for copy in copies:
        copy.start()
    slots = slots_of(levels, width)
    even = lax.axis_index("gx") % 2 == 0
    found = {}

    def find(j, t, pair):
        found[j, t] = pair[0]
        west_tiles[j, t], east_tiles[j, t] = pair

    for copy in copies[: tracers + 1]:
        copy.wait()
    for t, part in enumerate(slots):
        for i in range(tracers):
            find(i, t, window_tiles(lambda k: tracer[i, k], part))
        find(tracers + 2, t, window_tiles(lambda k: east[k], part))
    for copy in copies[tracers + 1 : -2]:
        copy.wait()
    floor = bottom[...] - lax.axis_index("gz") * levels
    signed = []
    for k in range(levels):
        is_wet = (mask[k] > 0) & (k < floor)
        wet[k] = jnp.where(is_wet, 1.0, 0.0)
        signed.append(jnp.where(is_wet, mixing[k], -mixing[k]))
    for t, part in enumerate(slots):
        both = window_tiles(lambda k: signed[k], part)
        find(tracers, t, [jnp.abs(b) for b in both])
        find(tracers + 1, t, [jnp.where(b > 0.0, 1.0, 0.0) for b in both])
        find(tracers + 3, t, window_tiles(lambda k: north[k], part))
    for t in range(len(slots)):
        for g in range(to_far.shape[0]):
            group = [found[g * GROUP + q, t] for q in range(GROUP)]
            to_far[g, t] = pack_group(group, even)
            to_near[g, t] = pack_group(group, jnp.logical_not(even))
    for copy in copies[-2:]:
        copy.wait()


def side_kernel(
    wet, vertical, mixing_vertical,
    down, up, from_first, from_last, pivots, ratios, couplings, weights, rims,
):
    vertical_statics(
        wet, vertical, mixing_vertical, down, up, from_first, from_last, pivots, ratios, couplings, weights, rims
    )


def interior_kernel(
    tracer, mixing, east, north, wet, weights, west_tiles, east_tiles, near, lateral, sums, near_edges, far_tiles
):
    levels = wet.shape[0]
    tracers = tracer.shape[0]
    arrays, tiles = east_tiles.shape[:2]
    even = lax.axis_index("gx") % 2 == 0
    own, received = {}, {(g, t): near[g, t] for g in range(near.shape[0]) for t in range(tiles)}
    for j in range(arrays):
        for t in range(tiles):
            own[j, t] = jnp.where(even, east_tiles[j, t], west_tiles[j, t])
            far_tiles[j, t] = jnp.where(even, west_tiles[j, t], east_tiles[j, t])
    done = window_results(own, received, even, tracers)
    coefficients = {k: lateral_coefficients(east[k], north[k], mixing[k], wet[k]) for k in range(levels)}
    planes = {(i, k): tracer[i, k] for k in range(levels) for i in range(tracers)}
    planes = lateral_substeps(planes, coefficients)
    for i, k in planes:
        lateral[i, k] = planes[i, k]
    for i, t in done:
        near_edges[i, t] = done[i, t]
    for i in range(tracers):
        for n in range(2):
            sums[n * tracers + i] = total([weights[n, k] * planes[i, k] for k in range(levels)])


def vertical_statics(
    wet_ref, vertical, mixing_vertical, down, up, from_first, from_last, pivots, ratios, couplings, weights, rims
):
    levels = wet_ref.shape[0]
    wet = [wet_ref[k] for k in range(levels)]
    both = [wet[k] * wet[k + 1] for k in range(levels - 1)]
    speeds = [vertical[k] * both[k] for k in range(levels - 1)]
    links = [mixing_vertical[k] * both[k] for k in range(levels - 1)]
    one = jnp.ones_like(wet[0])
    top_p = top_q = low_p = low_q = one
    pivot, ratio, upward = [None] * levels, [None] * levels, [None] * levels
    for k in range(levels - 1):
        next_q = top_p + links[k] * top_q
        next_p = next_q + links[k] * top_p
        inverse = 1.0 / next_q
        pivot[k] = top_q * inverse
        ratio[k] = links[k] * pivot[k]
        top_p, top_q = next_p, next_q
        m = levels - 2 - k
        next_q = low_p + links[m] * low_q
        next_p = next_q + links[m] * low_p
        low_inverse = 1.0 / next_q
        upward[m] = links[m] * low_q * low_inverse
        low_p, low_q = next_p, next_q
        if k % 6 == 5:
            top_p, top_q = top_p * inverse, one
            low_p, low_q = low_p * low_inverse, one
    last, first = [None] * levels, [None] * levels
    last[-1] = pivot[-1] = top_q / top_p
    first[0] = low_q / low_p
    for k in range(levels - 1):
        m = levels - 2 - k
        last[m] = ratio[m] * last[m + 1]
        first[k + 1] = upward[k] * first[k]
    link = wet[-1] * mixing_vertical[levels - 1]
    speed = wet[-1] * vertical[levels - 1]
    scale = 1.0 / (1.0 + link * last[-1])
    rim = [link * scale, jnp.maximum(speed, 0.0) * scale, jnp.minimum(speed, 0.0) * scale]
    rim += [wet[0] * low_p / low_q, last[0]]
    for k in range(levels):
        pivots[k], from_first[k], from_last[k] = pivot[k], first[k], last[k]
    for k in range(levels - 1):
        ratios[k], couplings[k] = ratio[k], links[k]
        down[k], up[k] = jnp.maximum(speeds[k], 0.0), jnp.minimum(speeds[k], 0.0)
    for n, column in enumerate((first, last)):
        for k in range(levels):
            weight = column[k]
            if k < levels - 1:
                weight = weight + jnp.minimum(speeds[k], 0.0) * (column[k] - column[k + 1])
            if k > 0:
                weight = weight + jnp.maximum(speeds[k - 1], 0.0) * (column[k - 1] - column[k])
            weights[n, k] = weight
    for n, value in enumerate(rim):
        rims[n] = value


def rim_kernel(far_tiles, far, near_edges, lateral, weights, sums, rims, edges, message):
    tracers, levels, _, width = lateral.shape
    odd = lax.axis_index("gx") % 2 == 1
    slots = slots_of(levels, width)
    arrays, tiles = far_tiles.shape[:2]
    lanes = lanes_of(rims[0])
    own = {(j, t): far_tiles[j, t] for j in range(arrays) for t in range(tiles)}
    received = {(g, t): far[g, t] for g in range(far.shape[0]) for t in range(tiles)}
    done = window_results(own, received, odd, tracers)
    from_far = places_of(rims[0], jnp.logical_not(odd)) < SUB
    edge = {(i, t): jnp.where(from_far, done[i, t], near_edges[i, t]) for i, t in done}
    at_rim = rim_lanes(lanes)
    placed = {(i, k): edge_at(edge[i, t], s) for t in range(tiles) for s, k in slots[t] for i in range(tracers)}
    for i in range(tracers):
        solved = [
            jnp.where(at_rim, total([weights[n, k] * placed[i, k] for k in range(levels)]), sums[n * tracers + i])
            for n in range(2)
        ]
        first = jnp.where(at_rim, placed[i, 0], lateral[i, 0])
        last = jnp.where(at_rim, placed[i, levels - 1], lateral[i, levels - 1])
        message[i] = rims[0] * solved[1] - rims[2] * last
        message[tracers + 2 + i] = rims[3] * solved[0]
        message[2 * tracers + 2 + i] = rims[3] * first
    message[tracers] = rims[0]
    message[tracers + 1] = rims[1]
    message[3 * tracers + 2] = rims[3]
    message[3 * tracers + 3] = rims[4]
    for i, t in edge:
        edges[i, t] = edge[i, t]


def rim_lanes(lanes):
    return (lanes < SUB) | (lanes >= lanes.shape[1] - SUB)


def edge_at(tile, slot):
    return rolled(tile, -SUB - SLOT * slot, 1)


def total(terms):
    while len(terms) > 1:
        terms = [sum(terms[n : n + 2][1:], terms[n]) for n in range(0, len(terms), 2)]
    return terms[0]


def block_kernel(lateral, edges, down, up, pivots, ratios, couplings, from_first, from_last, kept, base, gain):
    tracers, levels, _, width = lateral.shape
    slots = slots_of(levels, width)
    at_rim = rim_lanes(lanes_of(kept[0]))
    here = {
        (i, k): jnp.where(at_rim, edge_at(edges[i, t], s), lateral[i, k])
        for t in range(len(slots))
        for s, k in slots[t]
        for i in range(tracers)
    }
    values = {}
    for i in range(tracers):
        flux = [down[k] * here[i, k + 1] + up[k] * here[i, k] for k in range(levels - 1)]
        for k in range(levels):
            values[i, k] = here[i, k] if k == levels - 1 else here[i, k] + flux[k]
            if k > 0:
                values[i, k] = values[i, k] - flux[k - 1]
    for i in range(tracers):
        values[i, 0] = values[i, 0] * pivots[0]
    for k in range(1, levels):
        for i in range(tracers):
            values[i, k] = (values[i, k] + couplings[k - 1] * values[i, k - 1]) * pivots[k]
    for k in range(levels - 2, -1, -1):
        for i in range(tracers):
            values[i, k] = values[i, k] + ratios[k] * values[i, k + 1]
    z = lax.axis_index("gz")
    pair = [kept[i] for i in range(tracers)] + [kept[tracers]]
    top = [jnp.where((z == 1) | (z == 3), p, 0.0) for p in pair]
    low = [jnp.where((z == 0) | (z == 2), p, 0.0) for p in pair]
    top_gain = jnp.where(z == 2, 1.0, top[tracers])
    low_gain = jnp.where(z == 1, 1.0, low[tracers])
    for k in range(levels):
        gain[k] = low_gain * from_last[k] - top_gain * from_first[k]
        for i in range(tracers):
            base[i, k] = values[i, k] - top[i] * from_first[k] + low[i] * from_last[k]


def interface(upper, lower, tracers):
    heads, alpha, beta = upper[:tracers], upper[tracers], upper[tracers + 1]
    sums, rims, admit = lower[:tracers], lower[tracers : 2 * tracers], lower[2 * tracers]
    inverse = jnp.where(admit > 0.0, 1.0 / (admit + alpha), 0.0)
    flux = [(alpha * s + beta * r - admit * h) * inverse for s, r, h in zip(sums, rims, heads)]
    return flux, admit * alpha * inverse


def pair_kernel(own, other, merged, kept):
    tracers = kept.shape[0] - 1
    z = lax.axis_index("gz")
    lower_here = z % 2 == 1
    lower_pair = z >= 2
    upper, lower = [], []
    count = own.shape[0]
    for j in range(count):
        upper.append(jnp.where(lower_here, other[j], own[j]))
        lower.append(jnp.where(lower_here, own[j], other[j]))
    n = tracers + 2
    flux, gain = interface(upper[:n], lower[n:-1], tracers)
    across = jnp.where(lower_pair, upper[-1], lower[-1])
    gain = gain * across
    for i in range(tracers):
        kept[i] = flux[i]
    kept[tracers] = gain
    factor = across * jnp.where(lower_pair, upper[-2], lower[tracers])
    scale = 1.0 / (1.0 - factor * gain)
    for i in range(tracers):
        head = jnp.where(lower_pair, upper[n + i] + factor * flux[i], lower[i] - factor * flux[i])
        merged[i] = head * scale
    for i in range(tracers + 1):
        merged[tracers + i] = scale * (
            jnp.where(lower_pair, upper[n + tracers + i], lower[tracers + i] if i < 2 else 0.0)
        )


def final_kernel(own, other, base, gain, out, staged, sems):
    tracers, levels = base.shape[:2]
    lower_pair = lax.axis_index("gz") >= 2
    upper = [jnp.where(lower_pair, other[j], own[j]) for j in range(own.shape[0])]
    lower = [jnp.where(lower_pair, own[j], other[j]) for j in range(own.shape[0])]
    middle, _ = interface(upper[: tracers + 2], lower, tracers)
    copies = []
    for i in range(tracers):
        for k in range(levels):
            staged[i, k] = base[i, k] + middle[i] * gain[k]
        copies.append(pltpu.make_async_copy(staged.at[i], out.at[i], sems.at[i]))
        copies[i].start()
    for copy in copies:
        copy.wait()


def local(
    tracer, east_flow, north_flow, vertical_flow, mixing_lateral, mixing_vertical, sea_mask, bottom
):
    tracers, levels, rows, width = tracer.shape
    arrays = tracers + 4
    tiles = len(slots_of(levels, width))
    assert arrays == 2 * GROUP
    plane = (rows, width)
    block = (levels, rows, width)
    ring = lax.axis_size("gx")
    cells = levels * rows * width
    near_pairs = [(i, i ^ 1) for i in range(ring)]
    far_pairs = [(i, (i + 1) % ring if i % 2 else (i - 1) % ring) for i in range(ring)]

    tracer_here, mixing, east, north, wet, vertical, mixing_down, west_tiles, east_tiles, to_far, to_near = call(
        pack_kernel,
        [tracer.shape] + [block] * 6 + [(arrays, tiles) + plane] * 2 + [(2, tiles) + plane] * 2,
        20 * cells,
        tracer, mixing_lateral, east_flow, north_flow, sea_mask, bottom, vertical_flow, mixing_vertical,
        in_specs=[HBM] * 8,
        scratch=[
            pltpu.VMEM(block, jnp.int32),
            pltpu.VMEM(plane, jnp.int32),
            pltpu.SemaphoreType.DMA((tracers + 7,)),
        ],
    )
    far = lax.ppermute(to_far, "gx", far_pairs)
    near = lax.ppermute(to_near, "gx", near_pairs)
    down, up, from_first, from_last, pivots, ratios, couplings, weights, rims = call(
        side_kernel,
        [block] * 7 + [(2,) + block, (5,) + plane],
        50 * cells,
        wet, vertical, mixing_down,
    )
    lateral, sums, near_edges, far_tiles = call(
        interior_kernel,
        [tracer.shape, (2 * tracers,) + plane, (tracers, tiles) + plane, (arrays, tiles) + plane],
        100 * cells,
        tracer_here, mixing, east, north, wet, weights, west_tiles, east_tiles, near,
    )
    edges, message = call(
        rim_kernel,
        [(tracers, tiles) + plane, (3 * tracers + 4,) + plane],
        20 * cells,
        far_tiles, far, near_edges, lateral, weights, sums, rims,
    )
    other = lax.ppermute(message, "gz", [(i, i ^ 1) for i in range(4)])
    merged, kept = call(
        pair_kernel, [(2 * tracers + 1,) + plane, (tracers + 1,) + plane], cells, message, other
    )
    beyond = lax.ppermute(merged, "gz", [(i, i ^ 2) for i in range(4)])
    base, gain = call(
        block_kernel,
        [tracer.shape, block],
        40 * cells,
        lateral, edges, down, up, pivots, ratios, couplings, from_first, from_last, kept,
    )
    (result,) = call(
        final_kernel, [tracer.shape], 10 * cells, merged, beyond, base, gain,
        out_specs=[HBM],
        scratch=[pltpu.VMEM(tracer.shape, jnp.float32), pltpu.SemaphoreType.DMA((tracers,))],
    )
    return result


def solution(mesh):
    assert mesh.shape["gz"] == 4 and mesh.shape["gx"] % 2 == 0
    return jax.shard_map(
        local,
        mesh=mesh,
        in_specs=(
            P(None, "gz", None, "gx"),
            P("gz", None, "gx"),
            P("gz", None, "gx"),
            P("gz", None, "gx"),
            P("gz", None, "gx"),
            P("gz", None, "gx"),
            P("gz", None, "gx"),
            P(None, "gx"),
        ),
        out_specs=P(None, "gz", None, "gx"),
        check_vma=False,
    )
```

```python
import jax
import jax.numpy as jnp
from jax import lax
from jax.experimental import pallas as pl
from jax.experimental.pallas import tpu as pltpu
from jax.sharding import PartitionSpec as P

SUB = 3
SLOT = 3 * SUB
GROUP = SLOT // SUB

VMEM = pl.BlockSpec(memory_space=pltpu.VMEM)
HBM = pl.BlockSpec(memory_space=pltpu.HBM)


def call(kernel, shapes, flops, *operands, in_specs=None, out_specs=None, scratch=()):
    outs = [jax.ShapeDtypeStruct(s, jnp.float32) for s in shapes]
    if in_specs is not None:
        operands = [pltpu.with_memory_space_constraint(x, pltpu.HBM) if p is HBM else x for x, p in zip(operands, in_specs)]
    size = sum(o.size * o.dtype.itemsize for o in (*operands, *outs))
    return pl.pallas_call(
        kernel,
        out_shape=outs,
        in_specs=in_specs or [VMEM] * len(operands),
        out_specs=out_specs or [VMEM] * len(outs),
        scratch_shapes=list(scratch),
        compiler_params=pltpu.CompilerParams(vmem_limit_bytes=24 * 2**20),
        cost_estimate=pl.CostEstimate(flops=flops, bytes_accessed=size, transcendentals=0),
    )(*operands)


def rolled(plane, shift, axis):
    shift = shift % plane.shape[axis]
    return pltpu.roll(plane, shift, axis) if shift else plane


def lanes_of(plane):
    return lax.broadcasted_iota(jnp.int32, plane.shape, 1)


def places_of(plane, behind, ahead=0):
    factor = -(-512 // SLOT)
    assert all(n * factor >> 9 == n // SLOT for n in range(plane.shape[1] + 2 * SLOT))
    lane = lanes_of(plane) + jnp.where(behind, SLOT - SUB, 0) + (SLOT + ahead) % SLOT
    return lane - SLOT * ((lane * factor) >> 9)


def lateral_coefficients(east, north, mixing, wet):
    rows = east.shape[0]
    open_east = wet * rolled(wet, -1, 1)
    mean_east = 0.5 * (mixing + rolled(mixing, -1, 1))
    row = lax.broadcasted_iota(jnp.int32, wet.shape, 0)
    open_north = jnp.where(row < rows - 1, wet * rolled(wet, -1, 0), 0.0)
    mean_north = 0.5 * (mixing + rolled(mixing, -1, 0))
    return (
        open_east * (jnp.maximum(east, 0.0) + mean_east),
        open_east * (jnp.minimum(east, 0.0) - mean_east),
        open_north * (jnp.maximum(north, 0.0) + mean_north),
        open_north * (jnp.minimum(north, 0.0) - mean_north),
    )


def lateral_substeps(planes, coefficients):
    for _ in range(SUB):
        east = {q: rolled(c, -1, 1) for q, c in planes.items()}
        flux_east = {q: coefficients[q[1]][0] * c + coefficients[q[1]][1] * east[q] for q, c in planes.items()}
        flux_west = {q: rolled(f, 1, 1) for q, f in flux_east.items()}
        flux_north = {
            q: coefficients[q[1]][2] * c + coefficients[q[1]][3] * rolled(c, -1, 0) for q, c in planes.items()
        }
        planes = {
            q: c - ((flux_east[q] - flux_west[q]) + (flux_north[q] - rolled(flux_north[q], 1, 0)))
            for q, c in planes.items()
        }
    return planes


def stencil(east, north, mixing, wet, beside):
    rows = east.shape[0]
    wet_east, wet_west, mixing_east, mixing_west, east_west = beside
    open_east = wet * wet_east
    mean_east = 0.5 * (mixing + mixing_east)
    open_west = wet * wet_west
    mean_west = 0.5 * (mixing + mixing_west)
    row = lax.broadcasted_iota(jnp.int32, wet.shape, 0)
    open_north = jnp.where(row < rows - 1, wet * rolled(wet, -1, 0), 0.0)
    mean_north = 0.5 * (mixing + rolled(mixing, -1, 0))
    east_in = open_east * (mean_east - jnp.minimum(east, 0.0))
    east_out = open_east * (mean_east + jnp.maximum(east, 0.0))
    west_in = open_west * (mean_west + jnp.maximum(east_west, 0.0))
    west_out = open_west * (mean_west - jnp.minimum(east_west, 0.0))
    north_in = open_north * (mean_north - jnp.minimum(north, 0.0))
    north_out = open_north * (mean_north + jnp.maximum(north, 0.0))
    south_in = rolled(north_out, 1, 0)
    south_out = rolled(north_in, 1, 0)
    here = 1.0 - ((east_out + west_out) + (north_out + south_out))
    return here, east_in, west_in, north_in, south_in


def stencil_substeps(planes, weights, beside):
    for step in range(SUB):
        if step > 0:
            beside = {(q, d): rolled(c, d, 1) for q, c in planes.items() for d in (-1, 1)}
        planes = {
            q: (
                weights[q[1]][0] * c
                + weights[q[1]][3] * rolled(c, -1, 0)
                + weights[q[1]][4] * rolled(c, 1, 0)
            )
            + (weights[q[1]][1] * beside[q, -1] + weights[q[1]][2] * beside[q, 1])
            for q, c in planes.items()
        }
    return planes


def slots_of(levels, width):
    per_tile = width // SLOT
    tiles = -(-levels // per_tile)
    return [[(s, t * per_tile + s) for s in range(min(per_tile, levels - t * per_tile))] for t in range(tiles)]


def window_tiles(plane_of, slots):
    moved = [(slot, rolled(plane_of(level), SLOT * slot + SUB, 1)) for slot, level in slots]
    lane = lanes_of(moved[0][1])
    tiles = []
    for ahead in (0, SUB):
        parts = moved
        while len(parts) > 1:
            pairs = [parts[n : n + 2] for n in range(0, len(parts), 2)]
            parts = [
                p[0] if len(p) == 1 else (p[0][0], jnp.where(lane >= SLOT * p[1][0] - ahead, p[1][1], p[0][1]))
                for p in pairs
            ]
        tiles.append(parts[0][1])
    return tiles[0], jnp.where(lane >= lane.shape[1] - SUB, moved[0][1], tiles[1])


def pack_group(tiles, first_columns):
    place = places_of(tiles[0], first_columns)
    packed = tiles[0]
    for q, tile in enumerate(tiles[1:], 1):
        packed = jnp.where(place >= SUB * q, rolled(tile, SUB * q, 1), packed)
    return packed


def moved_pairs(tracers):
    mixing, wet, east = tracers, tracers + 1, tracers + 2
    return [(i, d) for i in range(tracers) for d in (-1, 1)] + [(wet, -1), (wet, 1), (mixing, -1), (mixing, 1), (east, 1)]


def window_results(own, received, behind, tracers, own_moved=None):
    tiles = [t for j, t in own if j == 0]

    def joined(j, t, d, mine):
        g, q = divmod(j, GROUP)
        theirs = places_of(mine, behind, -d) < SUB
        return jnp.where(theirs, rolled(received[g, t], d - SUB * q, 1), mine)

    windows = {(j, t): joined(j, t, 0, own[j, t]) for j, t in own}
    beside = {
        (j, d, t): rolled(windows[j, t], d, 1) if own_moved is None else joined(j, t, d, own_moved[j, d, t])
        for j, d in moved_pairs(tracers)
        for t in tiles
    }
    stencils = {
        t: stencil(
            *(windows[tracers + j, t] for j in (2, 3, 0, 1)), [beside[j, d, t] for j, d in moved_pairs(tracers)[2 * tracers :]]
        )
        for t in tiles
    }
    contents = {(j, t): windows[j, t] for j, t in own if j < tracers}
    return stencil_substeps(contents, stencils, {(q, d): beside[q[0], d, q[1]] for q in contents for d in (-1, 1)})


def pack_kernel(
    tracer_in, mixing_in, east_in, north_in, mask_in, bottom_in, vertical_in, mixing_vertical_in,
    tracer, mixing, east, north, wet, vertical, mixing_vertical, west_tiles, east_tiles, to_far, to_near, mask, bottom, sems,
):
    levels, _, width = mask.shape
    tracers = tracer.shape[0]
    pairs = [(tracer_in.at[i], tracer.at[i]) for i in range(tracers)]
    pairs += [(east_in, east), (bottom_in, bottom), (mask_in, mask), (north_in, north), (mixing_in, mixing)]
    pairs += [(vertical_in, vertical), (mixing_vertical_in, mixing_vertical)]
    copies = [pltpu.make_async_copy(source, target, sems.at[n]) for n, (source, target) in enumerate(pairs)]
    for copy in copies:
        copy.start()
    slots = slots_of(levels, width)
    even = lax.axis_index("gx") % 2 == 0
    found = {}

    def find(j, t, pair):
        found[j, t] = pair[0]
        west_tiles[j, t], east_tiles[j, t] = pair

    for copy in copies[: tracers + 1]:
        copy.wait()
    for t, part in enumerate(slots):
        for i in range(tracers):
            find(i, t, window_tiles(lambda k: tracer[i, k], part))
        find(tracers + 2, t, window_tiles(lambda k: east[k], part))
    for copy in copies[tracers + 1 : -2]:
        copy.wait()
    floor = bottom[...] - lax.axis_index("gz") * levels
    signed = []
    for k in range(levels):
        is_wet = (mask[k] > 0) & (k < floor)
        wet[k] = jnp.where(is_wet, 1.0, 0.0)
        signed.append(jnp.where(is_wet, mixing[k], -mixing[k]))
    for t, part in enumerate(slots):
        both = window_tiles(lambda k: signed[k], part)
        find(tracers, t, [jnp.abs(b) for b in both])
        find(tracers + 1, t, [jnp.where(b > 0.0, 1.0, 0.0) for b in both])
        find(tracers + 3, t, window_tiles(lambda k: north[k], part))
    for t in range(len(slots)):
        for g in range(to_far.shape[0]):
            group = [found[g * GROUP + q, t] for q in range(GROUP)]
            to_far[g, t] = pack_group(group, even)
            to_near[g, t] = pack_group(group, jnp.logical_not(even))
    for copy in copies[-2:]:
        copy.wait()


def side_kernel(
    wet, vertical, mixing_vertical, west_tiles, east_tiles,
    far_tiles, far_moved, down, up, from_first, from_last, pivots, ratios, couplings, weights, rims,
):
    arrays, tiles = east_tiles.shape[:2]
    even = lax.axis_index("gx") % 2 == 0
    own = {
        (j, t): jnp.where(even, west_tiles[j, t], east_tiles[j, t]) for j in range(arrays) for t in range(tiles)
    }
    moved = {
        (n, t): rolled(own[j, t], d, 1) for n, (j, d) in enumerate(moved_pairs(arrays - 4)) for t in range(tiles)
    }
    vertical_statics(
        wet, vertical, mixing_vertical, down, up, from_first, from_last, pivots, ratios, couplings, weights, rims
    )
    for j, t in own:
        far_tiles[j, t] = own[j, t]
    for n, t in moved:
        far_moved[n, t] = moved[n, t]


def interior_kernel(
    tracer, mixing, east, north, wet, weights, west_tiles, east_tiles, near,
    lateral, sums, near_edges,
):
    levels = wet.shape[0]
    tracers = tracer.shape[0]
    arrays, tiles = east_tiles.shape[:2]
    even = lax.axis_index("gx") % 2 == 0
    own, received = {}, {(g, t): near[g, t] for g in range(near.shape[0]) for t in range(tiles)}
    for j in range(arrays):
        for t in range(tiles):
            own[j, t] = jnp.where(even, east_tiles[j, t], west_tiles[j, t])
    done = window_results(own, received, even, tracers)
    coefficients = {k: lateral_coefficients(east[k], north[k], mixing[k], wet[k]) for k in range(levels)}
    planes = {(i, k): tracer[i, k] for k in range(levels) for i in range(tracers)}
    planes = lateral_substeps(planes, coefficients)
    for i, k in planes:
        lateral[i, k] = planes[i, k]
    for i, t in done:
        near_edges[i, t] = done[i, t]
    for i in range(tracers):
        for n in range(2):
            sums[n * tracers + i] = total([weights[n, k] * planes[i, k] for k in range(levels)])


def vertical_statics(
    wet_ref, vertical, mixing_vertical, down, up, from_first, from_last, pivots, ratios, couplings, weights, rims
):
    levels = wet_ref.shape[0]
    wet = [wet_ref[k] for k in range(levels)]
    both = [wet[k] * wet[k + 1] for k in range(levels - 1)]
    speeds = [vertical[k] * both[k] for k in range(levels - 1)]
    links = [mixing_vertical[k] * both[k] for k in range(levels - 1)]
    one = jnp.ones_like(wet[0])
    top_p = top_q = low_p = low_q = one
    pivot, ratio, upward = [None] * levels, [None] * levels, [None] * levels
    for k in range(levels - 1):
        next_q = top_p + links[k] * top_q
        next_p = next_q + links[k] * top_p
        inverse = 1.0 / next_q
        pivot[k] = top_q * inverse
        ratio[k] = links[k] * pivot[k]
        top_p, top_q = next_p, next_q
        m = levels - 2 - k
        next_q = low_p + links[m] * low_q
        next_p = next_q + links[m] * low_p
        low_inverse = 1.0 / next_q
        upward[m] = links[m] * low_q * low_inverse
        low_p, low_q = next_p, next_q
        if k % 6 == 5:
            top_p, top_q = top_p * inverse, one
            low_p, low_q = low_p * low_inverse, one
    last, first = [None] * levels, [None] * levels
    last[-1] = pivot[-1] = top_q / top_p
    first[0] = low_q / low_p
    for k in range(levels - 1):
        m = levels - 2 - k
        last[m] = ratio[m] * last[m + 1]
        first[k + 1] = upward[k] * first[k]
    link = wet[-1] * mixing_vertical[levels - 1]
    speed = wet[-1] * vertical[levels - 1]
    scale = 1.0 / (1.0 + link * last[-1])
    rim = [link * scale, jnp.maximum(speed, 0.0) * scale, jnp.minimum(speed, 0.0) * scale]
    rim += [wet[0] * low_p / low_q, last[0]]
    for k in range(levels):
        pivots[k], from_first[k], from_last[k] = pivot[k], first[k], last[k]
    for k in range(levels - 1):
        ratios[k], couplings[k] = ratio[k], links[k]
        down[k], up[k] = jnp.maximum(speeds[k], 0.0), jnp.minimum(speeds[k], 0.0)
    for n, column in enumerate((first, last)):
        for k in range(levels):
            weight = column[k]
            if k < levels - 1:
                weight = weight + jnp.minimum(speeds[k], 0.0) * (column[k] - column[k + 1])
            if k > 0:
                weight = weight + jnp.maximum(speeds[k - 1], 0.0) * (column[k - 1] - column[k])
            weights[n, k] = weight
    for n, value in enumerate(rim):
        rims[n] = value


def rim_kernel(far_tiles, far_moved, far, near_edges, lateral, weights, sums, rims, edges, message):
    tracers, levels, _, width = lateral.shape
    odd = lax.axis_index("gx") % 2 == 1
    slots = slots_of(levels, width)
    arrays, tiles = far_tiles.shape[:2]
    lanes = lanes_of(rims[0])
    own = {(j, t): far_tiles[j, t] for j in range(arrays) for t in range(tiles)}
    received = {(g, t): far[g, t] for g in range(far.shape[0]) for t in range(tiles)}
    moved = {(j, d, t): far_moved[n, t] for n, (j, d) in enumerate(moved_pairs(tracers)) for t in range(tiles)}
    done = window_results(own, received, odd, tracers, moved)
    from_far = places_of(rims[0], jnp.logical_not(odd)) < SUB
    edge = {(i, t): jnp.where(from_far, done[i, t], near_edges[i, t]) for i, t in done}
    at_rim = rim_lanes(lanes)
    placed = {(i, k): edge_at(edge[i, t], s) for t in range(tiles) for s, k in slots[t] for i in range(tracers)}
    for i in range(tracers):
        solved = [
            jnp.where(at_rim, total([weights[n, k] * placed[i, k] for k in range(levels)]), sums[n * tracers + i])
            for n in range(2)
        ]
        first = jnp.where(at_rim, placed[i, 0], lateral[i, 0])
        last = jnp.where(at_rim, placed[i, levels - 1], lateral[i, levels - 1])
        message[i] = rims[0] * solved[1] - rims[2] * last
        message[tracers + 2 + i] = rims[3] * solved[0]
        message[2 * tracers + 2 + i] = rims[3] * first
    message[tracers] = rims[0]
    message[tracers + 1] = rims[1]
    message[3 * tracers + 2] = rims[3]
    message[3 * tracers + 3] = rims[4]
    for i, t in edge:
        edges[i, t] = edge[i, t]


def rim_lanes(lanes):
    return (lanes < SUB) | (lanes >= lanes.shape[1] - SUB)


def edge_at(tile, slot):
    return rolled(tile, -SUB - SLOT * slot, 1)


def total(terms):
    while len(terms) > 1:
        terms = [sum(terms[n : n + 2][1:], terms[n]) for n in range(0, len(terms), 2)]
    return terms[0]


def block_kernel(lateral, edges, down, up, pivots, ratios, couplings, from_first, from_last, kept, base, gain):
    tracers, levels, _, width = lateral.shape
    slots = slots_of(levels, width)
    at_rim = rim_lanes(lanes_of(kept[0]))
    here = {
        (i, k): jnp.where(at_rim, edge_at(edges[i, t], s), lateral[i, k])
        for t in range(len(slots))
        for s, k in slots[t]
        for i in range(tracers)
    }
    values = {}
    for i in range(tracers):
        flux = [down[k] * here[i, k + 1] + up[k] * here[i, k] for k in range(levels - 1)]
        for k in range(levels):
            values[i, k] = here[i, k] if k == levels - 1 else here[i, k] + flux[k]
            if k > 0:
                values[i, k] = values[i, k] - flux[k - 1]
    for i in range(tracers):
        values[i, 0] = values[i, 0] * pivots[0]
    for k in range(1, levels):
        for i in range(tracers):
            values[i, k] = (values[i, k] + couplings[k - 1] * values[i, k - 1]) * pivots[k]
    for k in range(levels - 2, -1, -1):
        for i in range(tracers):
            values[i, k] = values[i, k] + ratios[k] * values[i, k + 1]
    z = lax.axis_index("gz")
    pair = [kept[i] for i in range(tracers)] + [kept[tracers]]
    top = [jnp.where((z == 1) | (z == 3), p, 0.0) for p in pair]
    low = [jnp.where((z == 0) | (z == 2), p, 0.0) for p in pair]
    top_gain = jnp.where(z == 2, 1.0, top[tracers])
    low_gain = jnp.where(z == 1, 1.0, low[tracers])
    for k in range(levels):
        gain[k] = low_gain * from_last[k] - top_gain * from_first[k]
        for i in range(tracers):
            base[i, k] = values[i, k] - top[i] * from_first[k] + low[i] * from_last[k]


def interface(upper, lower, tracers):
    heads, alpha, beta = upper[:tracers], upper[tracers], upper[tracers + 1]
    sums, rims, admit = lower[:tracers], lower[tracers : 2 * tracers], lower[2 * tracers]
    inverse = jnp.where(admit > 0.0, 1.0 / (admit + alpha), 0.0)
    flux = [(alpha * s + beta * r - admit * h) * inverse for s, r, h in zip(sums, rims, heads)]
    return flux, admit * alpha * inverse


def pair_kernel(own, other, merged, kept):
    tracers = kept.shape[0] - 1
    z = lax.axis_index("gz")
    lower_here = z % 2 == 1
    lower_pair = z >= 2
    upper, lower = [], []
    count = own.shape[0]
    for j in range(count):
        upper.append(jnp.where(lower_here, other[j], own[j]))
        lower.append(jnp.where(lower_here, own[j], other[j]))
    n = tracers + 2
    flux, gain = interface(upper[:n], lower[n:-1], tracers)
    across = jnp.where(lower_pair, upper[-1], lower[-1])
    gain = gain * across
    for i in range(tracers):
        kept[i] = flux[i]
    kept[tracers] = gain
    factor = across * jnp.where(lower_pair, upper[-2], lower[tracers])
    scale = 1.0 / (1.0 - factor * gain)
    for i in range(tracers):
        head = jnp.where(lower_pair, upper[n + i] + factor * flux[i], lower[i] - factor * flux[i])
        merged[i] = head * scale
    for i in range(tracers + 1):
        merged[tracers + i] = scale * (
            jnp.where(lower_pair, upper[n + tracers + i], lower[tracers + i] if i < 2 else 0.0)
        )


def final_kernel(own, other, base, gain, out, staged, sems):
    tracers, levels = base.shape[:2]
    lower_pair = lax.axis_index("gz") >= 2
    upper = [jnp.where(lower_pair, other[j], own[j]) for j in range(own.shape[0])]
    lower = [jnp.where(lower_pair, own[j], other[j]) for j in range(own.shape[0])]
    middle, _ = interface(upper[: tracers + 2], lower, tracers)
    copies = []
    for i in range(tracers):
        for k in range(levels):
            staged[i, k] = base[i, k] + middle[i] * gain[k]
        copies.append(pltpu.make_async_copy(staged.at[i], out.at[i], sems.at[i]))
        copies[i].start()
    for copy in copies:
        copy.wait()


def local(
    tracer, east_flow, north_flow, vertical_flow, mixing_lateral, mixing_vertical, sea_mask, bottom
):
    tracers, levels, rows, width = tracer.shape
    arrays = tracers + 4
    tiles = len(slots_of(levels, width))
    assert arrays == 2 * GROUP
    plane = (rows, width)
    block = (levels, rows, width)
    ring = lax.axis_size("gx")
    cells = levels * rows * width
    near_pairs = [(i, i ^ 1) for i in range(ring)]
    far_pairs = [(i, (i + 1) % ring if i % 2 else (i - 1) % ring) for i in range(ring)]

    tracer_here, mixing, east, north, wet, vertical, mixing_down, west_tiles, east_tiles, to_far, to_near = call(
        pack_kernel,
        [tracer.shape] + [block] * 6 + [(arrays, tiles) + plane] * 2 + [(2, tiles) + plane] * 2,
        20 * cells,
        tracer, mixing_lateral, east_flow, north_flow, sea_mask, bottom, vertical_flow, mixing_vertical,
        in_specs=[HBM] * 8,
        scratch=[
            pltpu.VMEM(block, jnp.int32),
            pltpu.VMEM(plane, jnp.int32),
            pltpu.SemaphoreType.DMA((tracers + 7,)),
        ],
    )
    far = lax.ppermute(to_far, "gx", far_pairs)
    near = lax.ppermute(to_near, "gx", near_pairs)
    far_tiles, far_moved, down, up, from_first, from_last, pivots, ratios, couplings, weights, rims = call(
        side_kernel,
        [(arrays, tiles) + plane, (len(moved_pairs(tracers)), tiles) + plane]
        + [block] * 7
        + [(2,) + block, (5,) + plane],
        50 * cells,
        wet, vertical, mixing_down, west_tiles, east_tiles,
    )
    lateral, sums, near_edges = call(
        interior_kernel,
        [tracer.shape, (2 * tracers,) + plane, (tracers, tiles) + plane],
        100 * cells,
        tracer_here, mixing, east, north, wet, weights, west_tiles, east_tiles, near,
    )
    edges, message = call(
        rim_kernel,
        [(tracers, tiles) + plane, (3 * tracers + 4,) + plane],
        20 * cells,
        far_tiles, far_moved, far, near_edges, lateral, weights, sums, rims,
    )
    other = lax.ppermute(message, "gz", [(i, i ^ 1) for i in range(4)])
    merged, kept = call(
        pair_kernel, [(2 * tracers + 1,) + plane, (tracers + 1,) + plane], cells, message, other
    )
    beyond = lax.ppermute(merged, "gz", [(i, i ^ 2) for i in range(4)])
    base, gain = call(
        block_kernel,
        [tracer.shape, block],
        40 * cells,
        lateral, edges, down, up, pivots, ratios, couplings, from_first, from_last, kept,
    )
    (result,) = call(
        final_kernel, [tracer.shape], 10 * cells, merged, beyond, base, gain,
        out_specs=[HBM],
        scratch=[pltpu.VMEM(tracer.shape, jnp.float32), pltpu.SemaphoreType.DMA((tracers,))],
    )
    return result


def solution(mesh):
    assert mesh.shape["gz"] == 4 and mesh.shape["gx"] % 2 == 0
    return jax.shard_map(
        local,
        mesh=mesh,
        in_specs=(
            P(None, "gz", None, "gx"),
            P("gz", None, "gx"),
            P("gz", None, "gx"),
            P("gz", None, "gx"),
            P("gz", None, "gx"),
            P("gz", None, "gx"),
            P("gz", None, "gx"),
            P(None, "gx"),
        ),
        out_specs=P(None, "gz", None, "gx"),
        check_vma=False,
    )
```

```python
import jax
import jax.numpy as jnp
from jax import lax
from jax.experimental import pallas as pl
from jax.experimental.pallas import tpu as pltpu
from jax.sharding import PartitionSpec as P

SUB = 3
SLOT = 3 * SUB
GROUP = SLOT // SUB

VMEM = pl.BlockSpec(memory_space=pltpu.VMEM)
HBM = pl.BlockSpec(memory_space=pltpu.HBM)


def call(kernel, shapes, flops, *operands, in_specs=None, out_specs=None, scratch=()):
    outs = [jax.ShapeDtypeStruct(s, jnp.float32) for s in shapes]
    if in_specs is not None:
        operands = [pltpu.with_memory_space_constraint(x, pltpu.HBM) if p is HBM else x for x, p in zip(operands, in_specs)]
    size = sum(o.size * o.dtype.itemsize for o in (*operands, *outs))
    return pl.pallas_call(
        kernel,
        out_shape=outs,
        in_specs=in_specs or [VMEM] * len(operands),
        out_specs=out_specs or [VMEM] * len(outs),
        scratch_shapes=list(scratch),
        compiler_params=pltpu.CompilerParams(vmem_limit_bytes=24 * 2**20),
        cost_estimate=pl.CostEstimate(flops=flops, bytes_accessed=size, transcendentals=0),
    )(*operands)


def rolled(plane, shift, axis):
    shift = shift % plane.shape[axis]
    return pltpu.roll(plane, shift, axis) if shift else plane


def lanes_of(plane):
    return lax.broadcasted_iota(jnp.int32, plane.shape, 1)


def places_of(plane, behind, ahead=0):
    factor = -(-512 // SLOT)
    assert all(n * factor >> 9 == n // SLOT for n in range(plane.shape[1] + 2 * SLOT))
    lane = lanes_of(plane) + jnp.where(behind, SLOT - SUB, 0) + (SLOT + ahead) % SLOT
    return lane - SLOT * ((lane * factor) >> 9)


def lateral_coefficients(east, north, mixing, wet):
    rows = east.shape[0]
    open_east = wet * rolled(wet, -1, 1)
    mean_east = 0.5 * (mixing + rolled(mixing, -1, 1))
    row = lax.broadcasted_iota(jnp.int32, wet.shape, 0)
    open_north = jnp.where(row < rows - 1, wet * rolled(wet, -1, 0), 0.0)
    mean_north = 0.5 * (mixing + rolled(mixing, -1, 0))
    return (
        open_east * (jnp.maximum(east, 0.0) + mean_east),
        open_east * (jnp.minimum(east, 0.0) - mean_east),
        open_north * (jnp.maximum(north, 0.0) + mean_north),
        open_north * (jnp.minimum(north, 0.0) - mean_north),
    )


def lateral_substeps(planes, coefficients):
    for _ in range(SUB):
        east = {q: rolled(c, -1, 1) for q, c in planes.items()}
        flux_east = {q: coefficients[q[1]][0] * c + coefficients[q[1]][1] * east[q] for q, c in planes.items()}
        flux_west = {q: rolled(f, 1, 1) for q, f in flux_east.items()}
        flux_north = {
            q: coefficients[q[1]][2] * c + coefficients[q[1]][3] * rolled(c, -1, 0) for q, c in planes.items()
        }
        planes = {
            q: c - ((flux_east[q] - flux_west[q]) + (flux_north[q] - rolled(flux_north[q], 1, 0)))
            for q, c in planes.items()
        }
    return planes


def stencil(east, north, mixing, wet, beside):
    rows = east.shape[0]
    wet_east, wet_west, mixing_east, mixing_west, east_west = beside
    open_east = wet * wet_east
    mean_east = 0.5 * (mixing + mixing_east)
    open_west = wet * wet_west
    mean_west = 0.5 * (mixing + mixing_west)
    row = lax.broadcasted_iota(jnp.int32, wet.shape, 0)
    open_north = jnp.where(row < rows - 1, wet * rolled(wet, -1, 0), 0.0)
    mean_north = 0.5 * (mixing + rolled(mixing, -1, 0))
    east_in = open_east * (mean_east - jnp.minimum(east, 0.0))
    east_out = open_east * (mean_east + jnp.maximum(east, 0.0))
    west_in = open_west * (mean_west + jnp.maximum(east_west, 0.0))
    west_out = open_west * (mean_west - jnp.minimum(east_west, 0.0))
    north_in = open_north * (mean_north - jnp.minimum(north, 0.0))
    north_out = open_north * (mean_north + jnp.maximum(north, 0.0))
    south_in = rolled(north_out, 1, 0)
    south_out = rolled(north_in, 1, 0)
    here = 1.0 - ((east_out + west_out) + (north_out + south_out))
    return here, east_in, west_in, north_in, south_in


def stencil_substeps(planes, weights, beside):
    for step in range(SUB):
        if step > 0:
            beside = {(q, d): rolled(c, d, 1) for q, c in planes.items() for d in (-1, 1)}
        planes = {
            q: (
                weights[q[1]][0] * c
                + weights[q[1]][3] * rolled(c, -1, 0)
                + weights[q[1]][4] * rolled(c, 1, 0)
            )
            + (weights[q[1]][1] * beside[q, -1] + weights[q[1]][2] * beside[q, 1])
            for q, c in planes.items()
        }
    return planes


def slots_of(levels, width):
    per_tile = width // SLOT
    tiles = -(-levels // per_tile)
    return [[(s, t * per_tile + s) for s in range(min(per_tile, levels - t * per_tile))] for t in range(tiles)]


def window_tiles(plane_of, slots):
    moved = [(slot, rolled(plane_of(level), SLOT * slot + SUB, 1)) for slot, level in slots]
    lane = lanes_of(moved[0][1])
    tiles = []
    for ahead in (0, SUB):
        parts = moved
        while len(parts) > 1:
            pairs = [parts[n : n + 2] for n in range(0, len(parts), 2)]
            parts = [
                p[0] if len(p) == 1 else (p[0][0], jnp.where(lane >= SLOT * p[1][0] - ahead, p[1][1], p[0][1]))
                for p in pairs
            ]
        tiles.append(parts[0][1])
    return tiles[0], jnp.where(lane >= lane.shape[1] - SUB, moved[0][1], tiles[1])


def pack_group(tiles, first_columns):
    place = places_of(tiles[0], first_columns)
    packed = tiles[0]
    for q, tile in enumerate(tiles[1:], 1):
        packed = jnp.where(place >= SUB * q, rolled(tile, SUB * q, 1), packed)
    return packed


def moved_pairs(tracers):
    mixing, wet, east = tracers, tracers + 1, tracers + 2
    return [(i, d) for i in range(tracers) for d in (-1, 1)] + [(wet, -1), (wet, 1), (mixing, -1), (mixing, 1), (east, 1)]


def window_results(own, received, behind, tracers, own_moved=None):
    tiles = [t for j, t in own if j == 0]

    def joined(j, t, d, mine):
        g, q = divmod(j, GROUP)
        theirs = places_of(mine, behind, -d) < SUB
        return jnp.where(theirs, rolled(received[g, t], d - SUB * q, 1), mine)

    windows = {(j, t): joined(j, t, 0, own[j, t]) for j, t in own}
    beside = {
        (j, d, t): rolled(windows[j, t], d, 1) if own_moved is None else joined(j, t, d, own_moved[j, d, t])
        for j, d in moved_pairs(tracers)
        for t in tiles
    }
    stencils = {
        t: stencil(
            *(windows[tracers + j, t] for j in (2, 3, 0, 1)), [beside[j, d, t] for j, d in moved_pairs(tracers)[2 * tracers :]]
        )
        for t in tiles
    }
    contents = {(j, t): windows[j, t] for j, t in own if j < tracers}
    return stencil_substeps(contents, stencils, {(q, d): beside[q[0], d, q[1]] for q in contents for d in (-1, 1)})


def pack_kernel(
    tracer_in, mixing_in, east_in, north_in, mask_in, bottom_in, vertical_in, mixing_vertical_in,
    tracer, mixing, east, north, wet, vertical, mixing_vertical, west_tiles, east_tiles, to_far, to_near, mask, bottom, sems,
):
    levels, _, width = mask.shape
    tracers = tracer.shape[0]
    assert tracers == 2
    pairs = [(tracer_in, tracer, 0), (east_in, east, 1), (bottom_in, bottom, 2), (mask_in, mask, 3), (north_in, north, 3)]
    pairs += [(mixing_in, mixing, 4), (vertical_in, vertical, 5), (mixing_vertical_in, mixing_vertical, 5)]
    copies = [pltpu.make_async_copy(source, target, sems.at[n]) for source, target, n in pairs]
    for copy in copies:
        copy.start()
    two_blocks = [pltpu.make_async_copy(tracer_in, tracer, sems.at[n]) for n in (3, 5)]
    slots = slots_of(levels, width)
    even = lax.axis_index("gx") % 2 == 0
    found = {}

    def find(j, t, pair):
        found[j, t] = pair[0]
        west_tiles[j, t], east_tiles[j, t] = pair

    copies[0].wait()
    copies[1].wait()
    for t, part in enumerate(slots):
        for i in range(tracers):
            find(i, t, window_tiles(lambda k: tracer[i, k], part))
        find(tracers + 2, t, window_tiles(lambda k: east[k], part))
    copies[2].wait()
    two_blocks[0].wait()
    copies[5].wait()
    floor = bottom[...] - lax.axis_index("gz") * levels
    signed = []
    for k in range(levels):
        is_wet = (mask[k] > 0) & (k < floor)
        wet[k] = jnp.where(is_wet, 1.0, 0.0)
        signed.append(jnp.where(is_wet, mixing[k], -mixing[k]))
    for t, part in enumerate(slots):
        both = window_tiles(lambda k: signed[k], part)
        find(tracers, t, [jnp.abs(b) for b in both])
        find(tracers + 1, t, [jnp.where(b > 0.0, 1.0, 0.0) for b in both])
        find(tracers + 3, t, window_tiles(lambda k: north[k], part))
    for t in range(len(slots)):
        for g in range(to_far.shape[0]):
            group = [found[g * GROUP + q, t] for q in range(GROUP)]
            to_far[g, t] = pack_group(group, even)
            to_near[g, t] = pack_group(group, jnp.logical_not(even))
    two_blocks[1].wait()


def side_kernel(
    wet, vertical, mixing_vertical, west_tiles, east_tiles,
    far_tiles, far_moved, down, up, from_first, from_last, pivots, ratios, couplings, weights, rims,
):
    arrays, tiles = east_tiles.shape[:2]
    even = lax.axis_index("gx") % 2 == 0
    own = {
        (j, t): jnp.where(even, west_tiles[j, t], east_tiles[j, t]) for j in range(arrays) for t in range(tiles)
    }
    moved = {
        (n, t): rolled(own[j, t], d, 1) for n, (j, d) in enumerate(moved_pairs(arrays - 4)) for t in range(tiles)
    }
    vertical_statics(
        wet, vertical, mixing_vertical, down, up, from_first, from_last, pivots, ratios, couplings, weights, rims
    )
    for j, t in own:
        far_tiles[j, t] = own[j, t]
    for n, t in moved:
        far_moved[n, t] = moved[n, t]


def interior_kernel(
    tracer, mixing, east, north, wet, weights, west_tiles, east_tiles, near,
    lateral, sums, near_edges,
):
    levels = wet.shape[0]
    tracers = tracer.shape[0]
    arrays, tiles = east_tiles.shape[:2]
    even = lax.axis_index("gx") % 2 == 0
    own, received = {}, {(g, t): near[g, t] for g in range(near.shape[0]) for t in range(tiles)}
    for j in range(arrays):
        for t in range(tiles):
            own[j, t] = jnp.where(even, east_tiles[j, t], west_tiles[j, t])
    done = window_results(own, received, even, tracers)
    coefficients = {k: lateral_coefficients(east[k], north[k], mixing[k], wet[k]) for k in range(levels)}
    planes = {(i, k): tracer[i, k] for k in range(levels) for i in range(tracers)}
    planes = lateral_substeps(planes, coefficients)
    for i, k in planes:
        lateral[i, k] = planes[i, k]
    for i, t in done:
        near_edges[i, t] = done[i, t]
    for i in range(tracers):
        for n in range(2):
            sums[n * tracers + i] = total([weights[n, k] * planes[i, k] for k in range(levels)])


def vertical_statics(
    wet_ref, vertical, mixing_vertical, down, up, from_first, from_last, pivots, ratios, couplings, weights, rims
):
    levels = wet_ref.shape[0]
    wet = [wet_ref[k] for k in range(levels)]
    both = [wet[k] * wet[k + 1] for k in range(levels - 1)]
    speeds = [vertical[k] * both[k] for k in range(levels - 1)]
    links = [mixing_vertical[k] * both[k] for k in range(levels - 1)]
    one = jnp.ones_like(wet[0])
    top_p = top_q = low_p = low_q = one
    pivot, ratio, upward = [None] * levels, [None] * levels, [None] * levels
    for k in range(levels - 1):
        next_q = top_p + links[k] * top_q
        next_p = next_q + links[k] * top_p
        inverse = 1.0 / next_q
        pivot[k] = top_q * inverse
        ratio[k] = links[k] * pivot[k]
        top_p, top_q = next_p, next_q
        m = levels - 2 - k
        next_q = low_p + links[m] * low_q
        next_p = next_q + links[m] * low_p
        low_inverse = 1.0 / next_q
        upward[m] = links[m] * low_q * low_inverse
        low_p, low_q = next_p, next_q
        if k % 6 == 5:
            top_p, top_q = top_p * inverse, one
            low_p, low_q = low_p * low_inverse, one
    last, first = [None] * levels, [None] * levels
    last[-1] = pivot[-1] = top_q / top_p
    first[0] = low_q / low_p
    for k in range(levels - 1):
        m = levels - 2 - k
        last[m] = ratio[m] * last[m + 1]
        first[k + 1] = upward[k] * first[k]
    link = wet[-1] * mixing_vertical[levels - 1]
    speed = wet[-1] * vertical[levels - 1]
    scale = 1.0 / (1.0 + link * last[-1])
    rim = [link * scale, jnp.maximum(speed, 0.0) * scale, jnp.minimum(speed, 0.0) * scale]
    rim += [wet[0] * low_p / low_q, last[0]]
    for k in range(levels):
        pivots[k], from_first[k], from_last[k] = pivot[k], first[k], last[k]
    for k in range(levels - 1):
        ratios[k], couplings[k] = ratio[k], links[k]
        down[k], up[k] = jnp.maximum(speeds[k], 0.0), jnp.minimum(speeds[k], 0.0)
    for n, column in enumerate((first, last)):
        for k in range(levels):
            weight = column[k]
            if k < levels - 1:
                weight = weight + jnp.minimum(speeds[k], 0.0) * (column[k] - column[k + 1])
            if k > 0:
                weight = weight + jnp.maximum(speeds[k - 1], 0.0) * (column[k - 1] - column[k])
            weights[n, k] = weight
    for n, value in enumerate(rim):
        rims[n] = value


def rim_kernel(far_tiles, far_moved, far, near_edges, lateral, weights, sums, rims, edges, message):
    tracers, levels, _, width = lateral.shape
    odd = lax.axis_index("gx") % 2 == 1
    slots = slots_of(levels, width)
    arrays, tiles = far_tiles.shape[:2]
    lanes = lanes_of(rims[0])
    own = {(j, t): far_tiles[j, t] for j in range(arrays) for t in range(tiles)}
    received = {(g, t): far[g, t] for g in range(far.shape[0]) for t in range(tiles)}
    moved = {(j, d, t): far_moved[n, t] for n, (j, d) in enumerate(moved_pairs(tracers)) for t in range(tiles)}
    done = window_results(own, received, odd, tracers, moved)
    from_far = places_of(rims[0], jnp.logical_not(odd)) < SUB
    edge = {(i, t): jnp.where(from_far, done[i, t], near_edges[i, t]) for i, t in done}
    at_rim = rim_lanes(lanes)
    placed = {(i, k): edge_at(edge[i, t], s) for t in range(tiles) for s, k in slots[t] for i in range(tracers)}
    for i in range(tracers):
        solved = [
            jnp.where(at_rim, total([weights[n, k] * placed[i, k] for k in range(levels)]), sums[n * tracers + i])
            for n in range(2)
        ]
        first = jnp.where(at_rim, placed[i, 0], lateral[i, 0])
        last = jnp.where(at_rim, placed[i, levels - 1], lateral[i, levels - 1])
        message[i] = rims[0] * solved[1] - rims[2] * last
        message[tracers + 2 + i] = rims[3] * solved[0]
        message[2 * tracers + 2 + i] = rims[3] * first
    message[tracers] = rims[0]
    message[tracers + 1] = rims[1]
    message[3 * tracers + 2] = rims[3]
    message[3 * tracers + 3] = rims[4]
    for i, t in edge:
        edges[i, t] = edge[i, t]


def rim_lanes(lanes):
    return (lanes < SUB) | (lanes >= lanes.shape[1] - SUB)


def edge_at(tile, slot):
    return rolled(tile, -SUB - SLOT * slot, 1)


def total(terms):
    while len(terms) > 1:
        terms = [sum(terms[n : n + 2][1:], terms[n]) for n in range(0, len(terms), 2)]
    return terms[0]


def block_kernel(lateral, edges, down, up, pivots, ratios, couplings, from_first, from_last, kept, base, gain):
    tracers, levels, _, width = lateral.shape
    slots = slots_of(levels, width)
    at_rim = rim_lanes(lanes_of(kept[0]))
    here = {
        (i, k): jnp.where(at_rim, edge_at(edges[i, t], s), lateral[i, k])
        for t in range(len(slots))
        for s, k in slots[t]
        for i in range(tracers)
    }
    values = {}
    for i in range(tracers):
        flux = [down[k] * here[i, k + 1] + up[k] * here[i, k] for k in range(levels - 1)]
        for k in range(levels):
            values[i, k] = here[i, k] if k == levels - 1 else here[i, k] + flux[k]
            if k > 0:
                values[i, k] = values[i, k] - flux[k - 1]
    for i in range(tracers):
        values[i, 0] = values[i, 0] * pivots[0]
    for k in range(1, levels):
        for i in range(tracers):
            values[i, k] = (values[i, k] + couplings[k - 1] * values[i, k - 1]) * pivots[k]
    for k in range(levels - 2, -1, -1):
        for i in range(tracers):
            values[i, k] = values[i, k] + ratios[k] * values[i, k + 1]
    z = lax.axis_index("gz")
    pair = [kept[i] for i in range(tracers)] + [kept[tracers]]
    top = [jnp.where((z == 1) | (z == 3), p, 0.0) for p in pair]
    low = [jnp.where((z == 0) | (z == 2), p, 0.0) for p in pair]
    top_gain = jnp.where(z == 2, 1.0, top[tracers])
    low_gain = jnp.where(z == 1, 1.0, low[tracers])
    for k in range(levels):
        gain[k] = low_gain * from_last[k] - top_gain * from_first[k]
        for i in range(tracers):
            base[i, k] = values[i, k] - top[i] * from_first[k] + low[i] * from_last[k]


def interface(upper, lower, tracers):
    heads, alpha, beta = upper[:tracers], upper[tracers], upper[tracers + 1]
    sums, rims, admit = lower[:tracers], lower[tracers : 2 * tracers], lower[2 * tracers]
    inverse = jnp.where(admit > 0.0, 1.0 / (admit + alpha), 0.0)
    flux = [(alpha * s + beta * r - admit * h) * inverse for s, r, h in zip(sums, rims, heads)]
    return flux, admit * alpha * inverse


def pair_kernel(own, other, merged, kept):
    tracers = kept.shape[0] - 1
    z = lax.axis_index("gz")
    lower_here = z % 2 == 1
    lower_pair = z >= 2
    upper, lower = [], []
    count = own.shape[0]
    for j in range(count):
        upper.append(jnp.where(lower_here, other[j], own[j]))
        lower.append(jnp.where(lower_here, own[j], other[j]))
    n = tracers + 2
    flux, gain = interface(upper[:n], lower[n:-1], tracers)
    across = jnp.where(lower_pair, upper[-1], lower[-1])
    gain = gain * across
    for i in range(tracers):
        kept[i] = flux[i]
    kept[tracers] = gain
    factor = across * jnp.where(lower_pair, upper[-2], lower[tracers])
    scale = 1.0 / (1.0 - factor * gain)
    for i in range(tracers):
        head = jnp.where(lower_pair, upper[n + i] + factor * flux[i], lower[i] - factor * flux[i])
        merged[i] = head * scale
    for i in range(tracers + 1):
        merged[tracers + i] = scale * (
            jnp.where(lower_pair, upper[n + tracers + i], lower[tracers + i] if i < 2 else 0.0)
        )


def final_kernel(own, other, base, gain, out, staged, sem):
    tracers, levels = base.shape[:2]
    lower_pair = lax.axis_index("gz") >= 2
    upper = [jnp.where(lower_pair, other[j], own[j]) for j in range(own.shape[0])]
    lower = [jnp.where(lower_pair, own[j], other[j]) for j in range(own.shape[0])]
    middle, _ = interface(upper[: tracers + 2], lower, tracers)
    for i in range(tracers):
        for k in range(levels):
            staged[i, k] = base[i, k] + middle[i] * gain[k]
        pltpu.make_async_copy(staged.at[i], out.at[i], sem).start()
    pltpu.make_async_copy(staged, out, sem).wait()


def local(
    tracer, east_flow, north_flow, vertical_flow, mixing_lateral, mixing_vertical, sea_mask, bottom
):
    tracers, levels, rows, width = tracer.shape
    arrays = tracers + 4
    tiles = len(slots_of(levels, width))
    assert arrays == 2 * GROUP
    plane = (rows, width)
    block = (levels, rows, width)
    ring = lax.axis_size("gx")
    cells = levels * rows * width
    near_pairs = [(i, i ^ 1) for i in range(ring)]
    far_pairs = [(i, (i + 1) % ring if i % 2 else (i - 1) % ring) for i in range(ring)]

    tracer_here, mixing, east, north, wet, vertical, mixing_down, west_tiles, east_tiles, to_far, to_near = call(
        pack_kernel,
        [tracer.shape] + [block] * 6 + [(arrays, tiles) + plane] * 2 + [(2, tiles) + plane] * 2,
        20 * cells,
        tracer, mixing_lateral, east_flow, north_flow, sea_mask, bottom, vertical_flow, mixing_vertical,
        in_specs=[HBM] * 8,
        scratch=[
            pltpu.VMEM(block, jnp.int32),
            pltpu.VMEM(plane, jnp.int32),
            pltpu.SemaphoreType.DMA((6,)),
        ],
    )
    far = lax.ppermute(to_far, "gx", far_pairs)
    near = lax.ppermute(to_near, "gx", near_pairs)
    far_tiles, far_moved, down, up, from_first, from_last, pivots, ratios, couplings, weights, rims = call(
        side_kernel,
        [(arrays, tiles) + plane, (len(moved_pairs(tracers)), tiles) + plane]
        + [block] * 7
        + [(2,) + block, (5,) + plane],
        50 * cells,
        wet, vertical, mixing_down, west_tiles, east_tiles,
    )
    lateral, sums, near_edges = call(
        interior_kernel,
        [tracer.shape, (2 * tracers,) + plane, (tracers, tiles) + plane],
        100 * cells,
        tracer_here, mixing, east, north, wet, weights, west_tiles, east_tiles, near,
    )
    edges, message = call(
        rim_kernel,
        [(tracers, tiles) + plane, (3 * tracers + 4,) + plane],
        20 * cells,
        far_tiles, far_moved, far, near_edges, lateral, weights, sums, rims,
    )
    other = lax.ppermute(message, "gz", [(i, i ^ 1) for i in range(4)])
    merged, kept = call(
        pair_kernel, [(2 * tracers + 1,) + plane, (tracers + 1,) + plane], cells, message, other
    )
    beyond = lax.ppermute(merged, "gz", [(i, i ^ 2) for i in range(4)])
    base, gain = call(
        block_kernel,
        [tracer.shape, block],
        40 * cells,
        lateral, edges, down, up, pivots, ratios, couplings, from_first, from_last, kept,
    )
    (result,) = call(
        final_kernel, [tracer.shape], 10 * cells, merged, beyond, base, gain,
        out_specs=[HBM],
        scratch=[pltpu.VMEM(tracer.shape, jnp.float32), pltpu.SemaphoreType.DMA],
    )
    return result


def solution(mesh):
    assert mesh.shape["gz"] == 4 and mesh.shape["gx"] % 2 == 0
    return jax.shard_map(
        local,
        mesh=mesh,
        in_specs=(
            P(None, "gz", None, "gx"),
            P("gz", None, "gx"),
            P("gz", None, "gx"),
            P("gz", None, "gx"),
            P("gz", None, "gx"),
            P("gz", None, "gx"),
            P("gz", None, "gx"),
            P(None, "gx"),
        ),
        out_specs=P(None, "gz", None, "gx"),
        check_vma=False,
    )
```

```python
import jax
import jax.numpy as jnp
from jax import lax
from jax.experimental import pallas as pl
from jax.experimental.pallas import tpu as pltpu
from jax.sharding import PartitionSpec as P

SUB = 3
SLOT = 3 * SUB
GROUP = SLOT // SUB

VMEM = pl.BlockSpec(memory_space=pltpu.VMEM)
HBM = pl.BlockSpec(memory_space=pltpu.HBM)


def call(kernel, shapes, flops, *operands, in_specs=None, out_specs=None, scratch=()):
    outs = [jax.ShapeDtypeStruct(s, jnp.float32) for s in shapes]
    if in_specs is not None:
        operands = [pltpu.with_memory_space_constraint(x, pltpu.HBM) if p is HBM else x for x, p in zip(operands, in_specs)]
    size = sum(o.size * o.dtype.itemsize for o in (*operands, *outs))
    return pl.pallas_call(
        kernel,
        out_shape=outs,
        in_specs=in_specs or [VMEM] * len(operands),
        out_specs=out_specs or [VMEM] * len(outs),
        scratch_shapes=list(scratch),
        compiler_params=pltpu.CompilerParams(vmem_limit_bytes=24 * 2**20),
        cost_estimate=pl.CostEstimate(flops=flops, bytes_accessed=size, transcendentals=0),
    )(*operands)


def rolled(plane, shift, axis):
    shift = shift % plane.shape[axis]
    return pltpu.roll(plane, shift, axis) if shift else plane


def lanes_of(plane):
    return lax.broadcasted_iota(jnp.int32, plane.shape, 1)


def places_of(plane, behind, ahead=0):
    factor = -(-512 // SLOT)
    assert all(n * factor >> 9 == n // SLOT for n in range(plane.shape[1] + 2 * SLOT))
    lane = lanes_of(plane) + jnp.where(behind, SLOT - SUB, 0) + (SLOT + ahead) % SLOT
    return lane - SLOT * ((lane * factor) >> 9)


def lateral_coefficients(east, north, mixing, wet):
    rows = east.shape[0]
    open_east = wet * rolled(wet, -1, 1)
    mean_east = 0.5 * (mixing + rolled(mixing, -1, 1))
    row = lax.broadcasted_iota(jnp.int32, wet.shape, 0)
    open_north = jnp.where(row < rows - 1, wet * rolled(wet, -1, 0), 0.0)
    mean_north = 0.5 * (mixing + rolled(mixing, -1, 0))
    return (
        open_east * (jnp.maximum(east, 0.0) + mean_east),
        open_east * (jnp.minimum(east, 0.0) - mean_east),
        open_north * (jnp.maximum(north, 0.0) + mean_north),
        open_north * (jnp.minimum(north, 0.0) - mean_north),
    )


def lateral_substeps(planes, coefficients):
    for _ in range(SUB):
        east = {q: rolled(c, -1, 1) for q, c in planes.items()}
        flux_east = {q: coefficients[q[1]][0] * c + coefficients[q[1]][1] * east[q] for q, c in planes.items()}
        flux_west = {q: rolled(f, 1, 1) for q, f in flux_east.items()}
        flux_north = {
            q: coefficients[q[1]][2] * c + coefficients[q[1]][3] * rolled(c, -1, 0) for q, c in planes.items()
        }
        planes = {
            q: c - ((flux_east[q] - flux_west[q]) + (flux_north[q] - rolled(flux_north[q], 1, 0)))
            for q, c in planes.items()
        }
    return planes


def stencil(east, north, mixing, wet, beside):
    rows = east.shape[0]
    wet_east, wet_west, mixing_east, mixing_west, east_west = beside
    open_east = wet * wet_east
    mean_east = 0.5 * (mixing + mixing_east)
    open_west = wet * wet_west
    mean_west = 0.5 * (mixing + mixing_west)
    row = lax.broadcasted_iota(jnp.int32, wet.shape, 0)
    open_north = jnp.where(row < rows - 1, wet * rolled(wet, -1, 0), 0.0)
    mean_north = 0.5 * (mixing + rolled(mixing, -1, 0))
    east_in = open_east * (mean_east - jnp.minimum(east, 0.0))
    east_out = open_east * (mean_east + jnp.maximum(east, 0.0))
    west_in = open_west * (mean_west + jnp.maximum(east_west, 0.0))
    west_out = open_west * (mean_west - jnp.minimum(east_west, 0.0))
    north_in = open_north * (mean_north - jnp.minimum(north, 0.0))
    north_out = open_north * (mean_north + jnp.maximum(north, 0.0))
    south_in = rolled(north_out, 1, 0)
    south_out = rolled(north_in, 1, 0)
    here = 1.0 - ((east_out + west_out) + (north_out + south_out))
    return here, east_in, west_in, north_in, south_in


def stencil_substeps(planes, weights, beside):
    for step in range(SUB):
        if step > 0:
            beside = {(q, d): rolled(c, d, 1) for q, c in planes.items() for d in (-1, 1)}
        planes = {
            q: (
                weights[q[1]][0] * c
                + weights[q[1]][3] * rolled(c, -1, 0)
                + weights[q[1]][4] * rolled(c, 1, 0)
            )
            + (weights[q[1]][1] * beside[q, -1] + weights[q[1]][2] * beside[q, 1])
            for q, c in planes.items()
        }
    return planes


def slots_of(levels, width):
    per_tile = width // SLOT
    tiles = -(-levels // per_tile)
    return [[(s, t * per_tile + s) for s in range(min(per_tile, levels - t * per_tile))] for t in range(tiles)]


def window_tiles(plane_of, slots):
    moved = [(slot, rolled(plane_of(level), SLOT * slot + SUB, 1)) for slot, level in slots]
    lane = lanes_of(moved[0][1])
    tiles = []
    for ahead in (0, SUB):
        parts = moved
        while len(parts) > 1:
            pairs = [parts[n : n + 2] for n in range(0, len(parts), 2)]
            parts = [
                p[0] if len(p) == 1 else (p[0][0], jnp.where(lane >= SLOT * p[1][0] - ahead, p[1][1], p[0][1]))
                for p in pairs
            ]
        tiles.append(parts[0][1])
    return tiles[0], jnp.where(lane >= lane.shape[1] - SUB, moved[0][1], tiles[1])


def pack_group(tiles, first_columns):
    place = places_of(tiles[0], first_columns)
    packed = tiles[0]
    for q, tile in enumerate(tiles[1:], 1):
        packed = jnp.where(place >= SUB * q, rolled(tile, SUB * q, 1), packed)
    return packed


def moved_pairs(tracers):
    mixing, wet, east = tracers, tracers + 1, tracers + 2
    return [(i, d) for i in range(tracers) for d in (-1, 1)] + [(wet, -1), (wet, 1), (mixing, -1), (mixing, 1), (east, 1)]


def window_results(own, received, behind, tracers, own_moved=None):
    tiles = [t for j, t in own if j == 0]

    def joined(j, t, d, mine):
        g, q = divmod(j, GROUP)
        theirs = places_of(mine, behind, -d) < SUB
        return jnp.where(theirs, rolled(received[g, t], d - SUB * q, 1), mine)

    windows = {(j, t): joined(j, t, 0, own[j, t]) for j, t in own}
    beside = {
        (j, d, t): rolled(windows[j, t], d, 1) if own_moved is None else joined(j, t, d, own_moved[j, d, t])
        for j, d in moved_pairs(tracers)
        for t in tiles
    }
    stencils = {
        t: stencil(
            *(windows[tracers + j, t] for j in (2, 3, 0, 1)), [beside[j, d, t] for j, d in moved_pairs(tracers)[2 * tracers :]]
        )
        for t in tiles
    }
    contents = {(j, t): windows[j, t] for j, t in own if j < tracers}
    return stencil_substeps(contents, stencils, {(q, d): beside[q[0], d, q[1]] for q in contents for d in (-1, 1)})


def pack_kernel(
    tracer_in, mixing_in, east_in, north_in, mask_in, bottom_in, vertical_in, mixing_vertical_in,
    tracer, mixing, east, north, wet, vertical, mixing_vertical, west_tiles, east_tiles, to_far, to_near, mask, bottom, sems,
):
    levels, _, width = mask.shape
    tracers = tracer.shape[0]
    assert tracers == 2
    pairs = [(tracer_in, tracer, 0), (east_in, east, 1), (bottom_in, bottom, 2), (mask_in, mask, 3), (mixing_in, mixing, 3)]
    pairs += [(north_in, north, 4), (vertical_in, vertical, 5), (mixing_vertical_in, mixing_vertical, 5)]
    copies = [pltpu.make_async_copy(source, target, sems.at[n]) for source, target, n in pairs]
    for copy in copies:
        copy.start()
    two_blocks = [pltpu.make_async_copy(tracer_in, tracer, sems.at[n]) for n in (3, 5)]
    slots = slots_of(levels, width)
    even = lax.axis_index("gx") % 2 == 0
    found = {}

    def find(j, t, pair):
        found[j, t] = pair[0]
        west_tiles[j, t], east_tiles[j, t] = pair

    copies[0].wait()
    copies[1].wait()
    for t, part in enumerate(slots):
        for i in range(tracers):
            find(i, t, window_tiles(lambda k: tracer[i, k], part))
        find(tracers + 2, t, window_tiles(lambda k: east[k], part))
    copies[2].wait()
    two_blocks[0].wait()
    copies[5].wait()
    floor = bottom[...] - lax.axis_index("gz") * levels
    signed = []
    for k in range(levels):
        is_wet = (mask[k] > 0) & (k < floor)
        wet[k] = jnp.where(is_wet, 1.0, 0.0)
        signed.append(jnp.where(is_wet, mixing[k], -mixing[k]))
    for t, part in enumerate(slots):
        both = window_tiles(lambda k: signed[k], part)
        find(tracers, t, [jnp.abs(b) for b in both])
        find(tracers + 1, t, [jnp.where(b > 0.0, 1.0, 0.0) for b in both])
        find(tracers + 3, t, window_tiles(lambda k: north[k], part))
    for t in range(len(slots)):
        for g in range(to_far.shape[0]):
            group = [found[g * GROUP + q, t] for q in range(GROUP)]
            to_far[g, t] = pack_group(group, even)
            to_near[g, t] = pack_group(group, jnp.logical_not(even))
    two_blocks[1].wait()


def side_kernel(
    wet, vertical, mixing_vertical, west_tiles, east_tiles,
    far_tiles, far_moved, down, up, from_first, from_last, pivots, ratios, couplings, weights, rims,
):
    arrays, tiles = east_tiles.shape[:2]
    even = lax.axis_index("gx") % 2 == 0
    own = {
        (j, t): jnp.where(even, west_tiles[j, t], east_tiles[j, t]) for j in range(arrays) for t in range(tiles)
    }
    moved = {
        (n, t): rolled(own[j, t], d, 1) for n, (j, d) in enumerate(moved_pairs(arrays - 4)) for t in range(tiles)
    }
    vertical_statics(
        wet, vertical, mixing_vertical, down, up, from_first, from_last, pivots, ratios, couplings, weights, rims
    )
    for j, t in own:
        far_tiles[j, t] = own[j, t]
    for n, t in moved:
        far_moved[n, t] = moved[n, t]


def interior_kernel(
    tracer, mixing, east, north, wet, weights, west_tiles, east_tiles, near,
    lateral, sums, near_edges,
):
    levels = wet.shape[0]
    tracers = tracer.shape[0]
    arrays, tiles = east_tiles.shape[:2]
    even = lax.axis_index("gx") % 2 == 0
    own, received = {}, {(g, t): near[g, t] for g in range(near.shape[0]) for t in range(tiles)}
    for j in range(arrays):
        for t in range(tiles):
            own[j, t] = jnp.where(even, east_tiles[j, t], west_tiles[j, t])
    done = window_results(own, received, even, tracers)
    coefficients = {k: lateral_coefficients(east[k], north[k], mixing[k], wet[k]) for k in range(levels)}
    planes = {(i, k): tracer[i, k] for k in range(levels) for i in range(tracers)}
    planes = lateral_substeps(planes, coefficients)
    for i, k in planes:
        lateral[i, k] = planes[i, k]
    for i, t in done:
        near_edges[i, t] = done[i, t]
    for i in range(tracers):
        for n in range(2):
            sums[n * tracers + i] = total([weights[n, k] * planes[i, k] for k in range(levels)])


def vertical_statics(
    wet_ref, vertical, mixing_vertical, down, up, from_first, from_last, pivots, ratios, couplings, weights, rims
):
    levels = wet_ref.shape[0]
    wet = [wet_ref[k] for k in range(levels)]
    both = [wet[k] * wet[k + 1] for k in range(levels - 1)]
    speeds = [vertical[k] * both[k] for k in range(levels - 1)]
    links = [mixing_vertical[k] * both[k] for k in range(levels - 1)]
    one = jnp.ones_like(wet[0])
    top_p = top_q = low_p = low_q = one
    pivot, ratio, upward = [None] * levels, [None] * levels, [None] * levels
    for k in range(levels - 1):
        next_q = top_p + links[k] * top_q
        next_p = next_q + links[k] * top_p
        inverse = 1.0 / next_q
        pivot[k] = top_q * inverse
        ratio[k] = links[k] * pivot[k]
        top_p, top_q = next_p, next_q
        m = levels - 2 - k
        next_q = low_p + links[m] * low_q
        next_p = next_q + links[m] * low_p
        low_inverse = 1.0 / next_q
        upward[m] = links[m] * low_q * low_inverse
        low_p, low_q = next_p, next_q
        if k % 6 == 5:
            top_p, top_q = top_p * inverse, one
            low_p, low_q = low_p * low_inverse, one
    last, first = [None] * levels, [None] * levels
    last[-1] = pivot[-1] = top_q / top_p
    first[0] = low_q / low_p
    for k in range(levels - 1):
        m = levels - 2 - k
        last[m] = ratio[m] * last[m + 1]
        first[k + 1] = upward[k] * first[k]
    link = wet[-1] * mixing_vertical[levels - 1]
    speed = wet[-1] * vertical[levels - 1]
    scale = 1.0 / (1.0 + link * last[-1])
    rim = [link * scale, jnp.maximum(speed, 0.0) * scale, jnp.minimum(speed, 0.0) * scale]
    rim += [wet[0] * low_p / low_q, last[0]]
    for k in range(levels):
        pivots[k], from_first[k], from_last[k] = pivot[k], first[k], last[k]
    for k in range(levels - 1):
        ratios[k], couplings[k] = ratio[k], links[k]
        down[k], up[k] = jnp.maximum(speeds[k], 0.0), jnp.minimum(speeds[k], 0.0)
    for n, column in enumerate((first, last)):
        for k in range(levels):
            weight = column[k]
            if k < levels - 1:
                weight = weight + jnp.minimum(speeds[k], 0.0) * (column[k] - column[k + 1])
            if k > 0:
                weight = weight + jnp.maximum(speeds[k - 1], 0.0) * (column[k - 1] - column[k])
            weights[n, k] = weight
    for n, value in enumerate(rim):
        rims[n] = value


def rim_kernel(far_tiles, far_moved, far, near_edges, lateral, weights, sums, rims, edges, message):
    tracers, levels, _, width = lateral.shape
    odd = lax.axis_index("gx") % 2 == 1
    slots = slots_of(levels, width)
    arrays, tiles = far_tiles.shape[:2]
    lanes = lanes_of(rims[0])
    own = {(j, t): far_tiles[j, t] for j in range(arrays) for t in range(tiles)}
    received = {(g, t): far[g, t] for g in range(far.shape[0]) for t in range(tiles)}
    moved = {(j, d, t): far_moved[n, t] for n, (j, d) in enumerate(moved_pairs(tracers)) for t in range(tiles)}
    done = window_results(own, received, odd, tracers, moved)
    from_far = places_of(rims[0], jnp.logical_not(odd)) < SUB
    edge = {(i, t): jnp.where(from_far, done[i, t], near_edges[i, t]) for i, t in done}
    at_rim = rim_lanes(lanes)
    placed = {(i, k): edge_at(edge[i, t], s) for t in range(tiles) for s, k in slots[t] for i in range(tracers)}
    for i in range(tracers):
        solved = [
            jnp.where(at_rim, total([weights[n, k] * placed[i, k] for k in range(levels)]), sums[n * tracers + i])
            for n in range(2)
        ]
        first = jnp.where(at_rim, placed[i, 0], lateral[i, 0])
        last = jnp.where(at_rim, placed[i, levels - 1], lateral[i, levels - 1])
        message[i] = rims[0] * solved[1] - rims[2] * last
        message[tracers + 2 + i] = rims[3] * solved[0]
        message[2 * tracers + 2 + i] = rims[3] * first
    message[tracers] = rims[0]
    message[tracers + 1] = rims[1]
    message[3 * tracers + 2] = rims[3]
    message[3 * tracers + 3] = rims[4]
    for i, t in edge:
        edges[i, t] = edge[i, t]


def rim_lanes(lanes):
    return (lanes < SUB) | (lanes >= lanes.shape[1] - SUB)


def edge_at(tile, slot):
    return rolled(tile, -SUB - SLOT * slot, 1)


def total(terms):
    while len(terms) > 1:
        terms = [sum(terms[n : n + 2][1:], terms[n]) for n in range(0, len(terms), 2)]
    return terms[0]


def block_kernel(lateral, edges, down, up, pivots, ratios, couplings, from_first, from_last, kept, base, gain):
    tracers, levels, _, width = lateral.shape
    slots = slots_of(levels, width)
    at_rim = rim_lanes(lanes_of(kept[0]))
    here = {
        (i, k): jnp.where(at_rim, edge_at(edges[i, t], s), lateral[i, k])
        for t in range(len(slots))
        for s, k in slots[t]
        for i in range(tracers)
    }
    values = {}
    for i in range(tracers):
        flux = [down[k] * here[i, k + 1] + up[k] * here[i, k] for k in range(levels - 1)]
        for k in range(levels):
            values[i, k] = here[i, k] if k == levels - 1 else here[i, k] + flux[k]
            if k > 0:
                values[i, k] = values[i, k] - flux[k - 1]
    for i in range(tracers):
        values[i, 0] = values[i, 0] * pivots[0]
    for k in range(1, levels):
        for i in range(tracers):
            values[i, k] = (values[i, k] + couplings[k - 1] * values[i, k - 1]) * pivots[k]
    for k in range(levels - 2, -1, -1):
        for i in range(tracers):
            values[i, k] = values[i, k] + ratios[k] * values[i, k + 1]
    z = lax.axis_index("gz")
    pair = [kept[i] for i in range(tracers)] + [kept[tracers]]
    top = [jnp.where((z == 1) | (z == 3), p, 0.0) for p in pair]
    low = [jnp.where((z == 0) | (z == 2), p, 0.0) for p in pair]
    top_gain = jnp.where(z == 2, 1.0, top[tracers])
    low_gain = jnp.where(z == 1, 1.0, low[tracers])
    for k in range(levels):
        gain[k] = low_gain * from_last[k] - top_gain * from_first[k]
        for i in range(tracers):
            base[i, k] = values[i, k] - top[i] * from_first[k] + low[i] * from_last[k]


def interface(upper, lower, tracers):
    heads, alpha, beta = upper[:tracers], upper[tracers], upper[tracers + 1]
    sums, rims, admit = lower[:tracers], lower[tracers : 2 * tracers], lower[2 * tracers]
    inverse = jnp.where(admit > 0.0, 1.0 / (admit + alpha), 0.0)
    flux = [(alpha * s + beta * r - admit * h) * inverse for s, r, h in zip(sums, rims, heads)]
    return flux, admit * alpha * inverse


def pair_kernel(own, other, merged, kept):
    tracers = kept.shape[0] - 1
    z = lax.axis_index("gz")
    lower_here = z % 2 == 1
    lower_pair = z >= 2
    upper, lower = [], []
    count = own.shape[0]
    for j in range(count):
        upper.append(jnp.where(lower_here, other[j], own[j]))
        lower.append(jnp.where(lower_here, own[j], other[j]))
    n = tracers + 2
    flux, gain = interface(upper[:n], lower[n:-1], tracers)
    across = jnp.where(lower_pair, upper[-1], lower[-1])
    gain = gain * across
    for i in range(tracers):
        kept[i] = flux[i]
    kept[tracers] = gain
    factor = across * jnp.where(lower_pair, upper[-2], lower[tracers])
    scale = 1.0 / (1.0 - factor * gain)
    for i in range(tracers):
        head = jnp.where(lower_pair, upper[n + i] + factor * flux[i], lower[i] - factor * flux[i])
        merged[i] = head * scale
    for i in range(tracers + 1):
        merged[tracers + i] = scale * (
            jnp.where(lower_pair, upper[n + tracers + i], lower[tracers + i] if i < 2 else 0.0)
        )


def final_kernel(own, other, base, gain, out, staged, sem):
    tracers, levels = base.shape[:2]
    lower_pair = lax.axis_index("gz") >= 2
    upper = [jnp.where(lower_pair, other[j], own[j]) for j in range(own.shape[0])]
    lower = [jnp.where(lower_pair, own[j], other[j]) for j in range(own.shape[0])]
    middle, _ = interface(upper[: tracers + 2], lower, tracers)
    for i in range(tracers):
        for k in range(levels):
            staged[i, k] = base[i, k] + middle[i] * gain[k]
        pltpu.make_async_copy(staged.at[i], out.at[i], sem).start()
    pltpu.make_async_copy(staged, out, sem).wait()


def local(
    tracer, east_flow, north_flow, vertical_flow, mixing_lateral, mixing_vertical, sea_mask, bottom
):
    tracers, levels, rows, width = tracer.shape
    arrays = tracers + 4
    tiles = len(slots_of(levels, width))
    assert arrays == 2 * GROUP
    plane = (rows, width)
    block = (levels, rows, width)
    ring = lax.axis_size("gx")
    cells = levels * rows * width
    near_pairs = [(i, i ^ 1) for i in range(ring)]
    far_pairs = [(i, (i + 1) % ring if i % 2 else (i - 1) % ring) for i in range(ring)]

    tracer_here, mixing, east, north, wet, vertical, mixing_down, west_tiles, east_tiles, to_far, to_near = call(
        pack_kernel,
        [tracer.shape] + [block] * 6 + [(arrays, tiles) + plane] * 2 + [(2, tiles) + plane] * 2,
        20 * cells,
        tracer, mixing_lateral, east_flow, north_flow, sea_mask, bottom, vertical_flow, mixing_vertical,
        in_specs=[HBM] * 8,
        scratch=[
            pltpu.VMEM(block, jnp.int32),
            pltpu.VMEM(plane, jnp.int32),
            pltpu.SemaphoreType.DMA((6,)),
        ],
    )
    far = lax.ppermute(to_far, "gx", far_pairs)
    near = lax.ppermute(to_near, "gx", near_pairs)
    far_tiles, far_moved, down, up, from_first, from_last, pivots, ratios, couplings, weights, rims = call(
        side_kernel,
        [(arrays, tiles) + plane, (len(moved_pairs(tracers)), tiles) + plane]
        + [block] * 7
        + [(2,) + block, (5,) + plane],
        50 * cells,
        wet, vertical, mixing_down, west_tiles, east_tiles,
    )
    lateral, sums, near_edges = call(
        interior_kernel,
        [tracer.shape, (2 * tracers,) + plane, (tracers, tiles) + plane],
        100 * cells,
        tracer_here, mixing, east, north, wet, weights, west_tiles, east_tiles, near,
    )
    edges, message = call(
        rim_kernel,
        [(tracers, tiles) + plane, (3 * tracers + 4,) + plane],
        20 * cells,
        far_tiles, far_moved, far, near_edges, lateral, weights, sums, rims,
    )
    other = lax.ppermute(message, "gz", [(i, i ^ 1) for i in range(4)])
    merged, kept = call(
        pair_kernel, [(2 * tracers + 1,) + plane, (tracers + 1,) + plane], cells, message, other
    )
    beyond = lax.ppermute(merged, "gz", [(i, i ^ 2) for i in range(4)])
    base, gain = call(
        block_kernel,
        [tracer.shape, block],
        40 * cells,
        lateral, edges, down, up, pivots, ratios, couplings, from_first, from_last, kept,
    )
    (result,) = call(
        final_kernel, [tracer.shape], 10 * cells, merged, beyond, base, gain,
        out_specs=[HBM],
        scratch=[pltpu.VMEM(tracer.shape, jnp.float32), pltpu.SemaphoreType.DMA],
    )
    return result


def solution(mesh):
    assert mesh.shape["gz"] == 4 and mesh.shape["gx"] % 2 == 0
    return jax.shard_map(
        local,
        mesh=mesh,
        in_specs=(
            P(None, "gz", None, "gx"),
            P("gz", None, "gx"),
            P("gz", None, "gx"),
            P("gz", None, "gx"),
            P("gz", None, "gx"),
            P("gz", None, "gx"),
            P("gz", None, "gx"),
            P(None, "gx"),
        ),
        out_specs=P(None, "gz", None, "gx"),
        check_vma=False,
    )
```

```python
import jax
import jax.numpy as jnp
from jax import lax
from jax.experimental import pallas as pl
from jax.experimental.pallas import tpu as pltpu
from jax.sharding import PartitionSpec as P

SUB = 3
SLOT = 3 * SUB
GROUP = SLOT // SUB

VMEM = pl.BlockSpec(memory_space=pltpu.VMEM)
HBM = pl.BlockSpec(memory_space=pltpu.HBM)


def call(kernel, shapes, flops, *operands, in_specs=None, out_specs=None, scratch=()):
    outs = [jax.ShapeDtypeStruct(s, jnp.float32) for s in shapes]
    if in_specs is not None:
        operands = [pltpu.with_memory_space_constraint(x, pltpu.HBM) if p is HBM else x for x, p in zip(operands, in_specs)]
    size = sum(o.size * o.dtype.itemsize for o in (*operands, *outs))
    return pl.pallas_call(
        kernel,
        out_shape=outs,
        in_specs=in_specs or [VMEM] * len(operands),
        out_specs=out_specs or [VMEM] * len(outs),
        scratch_shapes=list(scratch),
        compiler_params=pltpu.CompilerParams(vmem_limit_bytes=24 * 2**20),
        cost_estimate=pl.CostEstimate(flops=flops, bytes_accessed=size, transcendentals=0),
    )(*operands)


def rolled(plane, shift, axis):
    shift = shift % plane.shape[axis]
    return pltpu.roll(plane, shift, axis) if shift else plane


def lanes_of(plane):
    return lax.broadcasted_iota(jnp.int32, plane.shape, 1)


def places_of(plane, behind, ahead=0):
    factor = -(-512 // SLOT)
    assert all(n * factor >> 9 == n // SLOT for n in range(plane.shape[1] + 2 * SLOT))
    lane = lanes_of(plane) + jnp.where(behind, SLOT - SUB, 0) + (SLOT + ahead) % SLOT
    return lane - SLOT * ((lane * factor) >> 9)


def lateral_coefficients(east, north, mixing, wet):
    rows = east.shape[0]
    open_east = wet * rolled(wet, -1, 1)
    mean_east = 0.5 * (mixing + rolled(mixing, -1, 1))
    row = lax.broadcasted_iota(jnp.int32, wet.shape, 0)
    open_north = jnp.where(row < rows - 1, wet * rolled(wet, -1, 0), 0.0)
    mean_north = 0.5 * (mixing + rolled(mixing, -1, 0))
    return (
        open_east * (jnp.maximum(east, 0.0) + mean_east),
        open_east * (jnp.minimum(east, 0.0) - mean_east),
        open_north * (jnp.maximum(north, 0.0) + mean_north),
        open_north * (jnp.minimum(north, 0.0) - mean_north),
    )


def lateral_substeps(planes, coefficients):
    for _ in range(SUB):
        east = {q: rolled(c, -1, 1) for q, c in planes.items()}
        flux_east = {q: coefficients[q[1]][0] * c + coefficients[q[1]][1] * east[q] for q, c in planes.items()}
        flux_west = {q: rolled(f, 1, 1) for q, f in flux_east.items()}
        flux_north = {
            q: coefficients[q[1]][2] * c + coefficients[q[1]][3] * rolled(c, -1, 0) for q, c in planes.items()
        }
        planes = {
            q: c - ((flux_east[q] - flux_west[q]) + (flux_north[q] - rolled(flux_north[q], 1, 0)))
            for q, c in planes.items()
        }
    return planes


def stencil(east, north, mixing, wet, beside):
    rows = east.shape[0]
    wet_east, wet_west, mixing_east, mixing_west, east_west = beside
    open_east = wet * wet_east
    mean_east = 0.5 * (mixing + mixing_east)
    open_west = wet * wet_west
    mean_west = 0.5 * (mixing + mixing_west)
    row = lax.broadcasted_iota(jnp.int32, wet.shape, 0)
    open_north = jnp.where(row < rows - 1, wet * rolled(wet, -1, 0), 0.0)
    mean_north = 0.5 * (mixing + rolled(mixing, -1, 0))
    east_in = open_east * (mean_east - jnp.minimum(east, 0.0))
    east_out = open_east * (mean_east + jnp.maximum(east, 0.0))
    west_in = open_west * (mean_west + jnp.maximum(east_west, 0.0))
    west_out = open_west * (mean_west - jnp.minimum(east_west, 0.0))
    north_in = open_north * (mean_north - jnp.minimum(north, 0.0))
    north_out = open_north * (mean_north + jnp.maximum(north, 0.0))
    south_in = rolled(north_out, 1, 0)
    south_out = rolled(north_in, 1, 0)
    here = 1.0 - ((east_out + west_out) + (north_out + south_out))
    return here, east_in, west_in, north_in, south_in


def stencil_substeps(planes, weights, beside):
    for step in range(SUB):
        if step > 0:
            beside = {(q, d): rolled(c, d, 1) for q, c in planes.items() for d in (-1, 1)}
        planes = {
            q: (
                weights[q[1]][0] * c
                + weights[q[1]][3] * rolled(c, -1, 0)
                + weights[q[1]][4] * rolled(c, 1, 0)
            )
            + (weights[q[1]][1] * beside[q, -1] + weights[q[1]][2] * beside[q, 1])
            for q, c in planes.items()
        }
    return planes


def slots_of(levels, width):
    per_tile = width // SLOT
    tiles = -(-levels // per_tile)
    return [[(s, t * per_tile + s) for s in range(min(per_tile, levels - t * per_tile))] for t in range(tiles)]


def window_tiles(plane_of, slots):
    moved = [(slot, rolled(plane_of(level), SLOT * slot + SUB, 1)) for slot, level in slots]
    lane = lanes_of(moved[0][1])
    tiles = []
    for ahead in (0, SUB):
        parts = moved
        while len(parts) > 1:
            pairs = [parts[n : n + 2] for n in range(0, len(parts), 2)]
            parts = [
                p[0] if len(p) == 1 else (p[0][0], jnp.where(lane >= SLOT * p[1][0] - ahead, p[1][1], p[0][1]))
                for p in pairs
            ]
        tiles.append(parts[0][1])
    return tiles[0], jnp.where(lane >= lane.shape[1] - SUB, moved[0][1], tiles[1])


def pack_group(tiles, first_columns):
    place = places_of(tiles[0], first_columns)
    packed = tiles[0]
    for q, tile in enumerate(tiles[1:], 1):
        packed = jnp.where(place >= SUB * q, rolled(tile, SUB * q, 1), packed)
    return packed


def moved_pairs(tracers):
    mixing, wet, east = tracers, tracers + 1, tracers + 2
    return [(i, d) for i in range(tracers) for d in (-1, 1)] + [(wet, -1), (wet, 1), (mixing, -1), (mixing, 1), (east, 1)]


def window_results(own, received, behind, tracers, own_moved=None):
    tiles = [t for j, t in own if j == 0]

    def joined(j, t, d, mine):
        g, q = divmod(j, GROUP)
        theirs = places_of(mine, behind, -d) < SUB
        return jnp.where(theirs, rolled(received[g, t], d - SUB * q, 1), mine)

    windows = {(j, t): joined(j, t, 0, own[j, t]) for j, t in own}
    beside = {
        (j, d, t): rolled(windows[j, t], d, 1) if own_moved is None else joined(j, t, d, own_moved[j, d, t])
        for j, d in moved_pairs(tracers)
        for t in tiles
    }
    stencils = {
        t: stencil(
            *(windows[tracers + j, t] for j in (2, 3, 0, 1)), [beside[j, d, t] for j, d in moved_pairs(tracers)[2 * tracers :]]
        )
        for t in tiles
    }
    contents = {(j, t): windows[j, t] for j, t in own if j < tracers}
    return stencil_substeps(contents, stencils, {(q, d): beside[q[0], d, q[1]] for q in contents for d in (-1, 1)})


def pack_kernel(
    tracer_in, mixing_in, east_in, north_in, mask_in, bottom_in, vertical_in, mixing_vertical_in,
    tracer, mixing, east, north, wet, vertical, mixing_vertical, west_tiles, east_tiles, to_far, to_near, mask, bottom, sems,
):
    levels, _, width = mask.shape
    tracers = tracer.shape[0]
    assert tracers == 2
    pairs = [(bottom_in, bottom, 2), (tracer_in, tracer, 0), (east_in, east, 1), (mask_in, mask, 3), (mixing_in, mixing, 3)]
    pairs += [(north_in, north, 4), (vertical_in, vertical, 5), (mixing_vertical_in, mixing_vertical, 5)]
    copies = [pltpu.make_async_copy(source, target, sems.at[n]) for source, target, n in pairs]
    for copy in copies:
        copy.start()
    two_blocks = [pltpu.make_async_copy(tracer_in, tracer, sems.at[n]) for n in (3, 5)]
    slots = slots_of(levels, width)
    even = lax.axis_index("gx") % 2 == 0
    found = {}

    def find(j, t, pair):
        found[j, t] = pair[0]
        west_tiles[j, t], east_tiles[j, t] = pair

    copies[1].wait()
    copies[2].wait()
    for t, part in enumerate(slots):
        for i in range(tracers):
            find(i, t, window_tiles(lambda k: tracer[i, k], part))
        find(tracers + 2, t, window_tiles(lambda k: east[k], part))
    copies[0].wait()
    two_blocks[0].wait()
    copies[5].wait()
    floor = bottom[...] - lax.axis_index("gz") * levels
    signed = []
    for k in range(levels):
        is_wet = (mask[k] > 0) & (k < floor)
        wet[k] = jnp.where(is_wet, 1.0, 0.0)
        signed.append(jnp.where(is_wet, mixing[k], -mixing[k]))
    for t, part in enumerate(slots):
        both = window_tiles(lambda k: signed[k], part)
        find(tracers, t, [jnp.abs(b) for b in both])
        find(tracers + 1, t, [jnp.where(b > 0.0, 1.0, 0.0) for b in both])
        find(tracers + 3, t, window_tiles(lambda k: north[k], part))
    for t in range(len(slots)):
        for g in range(to_far.shape[0]):
            group = [found[g * GROUP + q, t] for q in range(GROUP)]
            to_far[g, t] = pack_group(group, even)
            to_near[g, t] = pack_group(group, jnp.logical_not(even))
    two_blocks[1].wait()


def side_kernel(
    wet, vertical, mixing_vertical, west_tiles, east_tiles,
    far_tiles, far_moved, down, up, from_first, from_last, pivots, ratios, couplings, weights, rims,
):
    arrays, tiles = east_tiles.shape[:2]
    even = lax.axis_index("gx") % 2 == 0
    own = {
        (j, t): jnp.where(even, west_tiles[j, t], east_tiles[j, t]) for j in range(arrays) for t in range(tiles)
    }
    moved = {
        (n, t): rolled(own[j, t], d, 1) for n, (j, d) in enumerate(moved_pairs(arrays - 4)) for t in range(tiles)
    }
    vertical_statics(
        wet, vertical, mixing_vertical, down, up, from_first, from_last, pivots, ratios, couplings, weights, rims
    )
    for j, t in own:
        far_tiles[j, t] = own[j, t]
    for n, t in moved:
        far_moved[n, t] = moved[n, t]


def interior_kernel(
    tracer, mixing, east, north, wet, weights, west_tiles, east_tiles, near,
    lateral, sums, near_edges,
):
    levels = wet.shape[0]
    tracers = tracer.shape[0]
    arrays, tiles = east_tiles.shape[:2]
    even = lax.axis_index("gx") % 2 == 0
    own, received = {}, {(g, t): near[g, t] for g in range(near.shape[0]) for t in range(tiles)}
    for j in range(arrays):
        for t in range(tiles):
            own[j, t] = jnp.where(even, east_tiles[j, t], west_tiles[j, t])
    done = window_results(own, received, even, tracers)
    coefficients = {k: lateral_coefficients(east[k], north[k], mixing[k], wet[k]) for k in range(levels)}
    planes = {(i, k): tracer[i, k] for k in range(levels) for i in range(tracers)}
    planes = lateral_substeps(planes, coefficients)
    for i, k in planes:
        lateral[i, k] = planes[i, k]
    for i, t in done:
        near_edges[i, t] = done[i, t]
    for i in range(tracers):
        for n in range(2):
            sums[n * tracers + i] = total([weights[n, k] * planes[i, k] for k in range(levels)])


def vertical_statics(
    wet_ref, vertical, mixing_vertical, down, up, from_first, from_last, pivots, ratios, couplings, weights, rims
):
    levels = wet_ref.shape[0]
    wet = [wet_ref[k] for k in range(levels)]
    both = [wet[k] * wet[k + 1] for k in range(levels - 1)]
    speeds = [vertical[k] * both[k] for k in range(levels - 1)]
    links = [mixing_vertical[k] * both[k] for k in range(levels - 1)]
    one = jnp.ones_like(wet[0])
    top_p = top_q = low_p = low_q = one
    pivot, ratio, upward = [None] * levels, [None] * levels, [None] * levels
    for k in range(levels - 1):
        next_q = top_p + links[k] * top_q
        next_p = next_q + links[k] * top_p
        inverse = 1.0 / next_q
        pivot[k] = top_q * inverse
        ratio[k] = links[k] * pivot[k]
        top_p, top_q = next_p, next_q
        m = levels - 2 - k
        next_q = low_p + links[m] * low_q
        next_p = next_q + links[m] * low_p
        low_inverse = 1.0 / next_q
        upward[m] = links[m] * low_q * low_inverse
        low_p, low_q = next_p, next_q
        if k % 6 == 5:
            top_p, top_q = top_p * inverse, one
            low_p, low_q = low_p * low_inverse, one
    last, first = [None] * levels, [None] * levels
    last[-1] = pivot[-1] = top_q / top_p
    first[0] = low_q / low_p
    for k in range(levels - 1):
        m = levels - 2 - k
        last[m] = ratio[m] * last[m + 1]
        first[k + 1] = upward[k] * first[k]
    link = wet[-1] * mixing_vertical[levels - 1]
    speed = wet[-1] * vertical[levels - 1]
    scale = 1.0 / (1.0 + link * last[-1])
    rim = [link * scale, jnp.maximum(speed, 0.0) * scale, jnp.minimum(speed, 0.0) * scale]
    rim += [wet[0] * low_p / low_q, last[0]]
    for k in range(levels):
        pivots[k], from_first[k], from_last[k] = pivot[k], first[k], last[k]
    for k in range(levels - 1):
        ratios[k], couplings[k] = ratio[k], links[k]
        down[k], up[k] = jnp.maximum(speeds[k], 0.0), jnp.minimum(speeds[k], 0.0)
    for n, column in enumerate((first, last)):
        for k in range(levels):
            weight = column[k]
            if k < levels - 1:
                weight = weight + jnp.minimum(speeds[k], 0.0) * (column[k] - column[k + 1])
            if k > 0:
                weight = weight + jnp.maximum(speeds[k - 1], 0.0) * (column[k - 1] - column[k])
            weights[n, k] = weight
    for n, value in enumerate(rim):
        rims[n] = value


def rim_kernel(far_tiles, far_moved, far, near_edges, lateral, weights, sums, rims, edges, message):
    tracers, levels, _, width = lateral.shape
    odd = lax.axis_index("gx") % 2 == 1
    slots = slots_of(levels, width)
    arrays, tiles = far_tiles.shape[:2]
    lanes = lanes_of(rims[0])
    own = {(j, t): far_tiles[j, t] for j in range(arrays) for t in range(tiles)}
    received = {(g, t): far[g, t] for g in range(far.shape[0]) for t in range(tiles)}
    moved = {(j, d, t): far_moved[n, t] for n, (j, d) in enumerate(moved_pairs(tracers)) for t in range(tiles)}
    done = window_results(own, received, odd, tracers, moved)
    from_far = places_of(rims[0], jnp.logical_not(odd)) < SUB
    edge = {(i, t): jnp.where(from_far, done[i, t], near_edges[i, t]) for i, t in done}
    at_rim = rim_lanes(lanes)
    placed = {(i, k): edge_at(edge[i, t], s) for t in range(tiles) for s, k in slots[t] for i in range(tracers)}
    for i in range(tracers):
        solved = [
            jnp.where(at_rim, total([weights[n, k] * placed[i, k] for k in range(levels)]), sums[n * tracers + i])
            for n in range(2)
        ]
        first = jnp.where(at_rim, placed[i, 0], lateral[i, 0])
        last = jnp.where(at_rim, placed[i, levels - 1], lateral[i, levels - 1])
        message[i] = rims[0] * solved[1] - rims[2] * last
        message[tracers + 2 + i] = rims[3] * solved[0]
        message[2 * tracers + 2 + i] = rims[3] * first
    message[tracers] = rims[0]
    message[tracers + 1] = rims[1]
    message[3 * tracers + 2] = rims[3]
    message[3 * tracers + 3] = rims[4]
    for i, t in edge:
        edges[i, t] = edge[i, t]


def rim_lanes(lanes):
    return (lanes < SUB) | (lanes >= lanes.shape[1] - SUB)


def edge_at(tile, slot):
    return rolled(tile, -SUB - SLOT * slot, 1)


def total(terms):
    while len(terms) > 1:
        terms = [sum(terms[n : n + 2][1:], terms[n]) for n in range(0, len(terms), 2)]
    return terms[0]


def block_kernel(lateral, edges, down, up, pivots, ratios, couplings, from_first, from_last, kept, base, gain):
    tracers, levels, _, width = lateral.shape
    slots = slots_of(levels, width)
    at_rim = rim_lanes(lanes_of(kept[0]))
    here = {
        (i, k): jnp.where(at_rim, edge_at(edges[i, t], s), lateral[i, k])
        for t in range(len(slots))
        for s, k in slots[t]
        for i in range(tracers)
    }
    values = {}
    for i in range(tracers):
        flux = [down[k] * here[i, k + 1] + up[k] * here[i, k] for k in range(levels - 1)]
        for k in range(levels):
            values[i, k] = here[i, k] if k == levels - 1 else here[i, k] + flux[k]
            if k > 0:
                values[i, k] = values[i, k] - flux[k - 1]
    for i in range(tracers):
        values[i, 0] = values[i, 0] * pivots[0]
    for k in range(1, levels):
        for i in range(tracers):
            values[i, k] = (values[i, k] + couplings[k - 1] * values[i, k - 1]) * pivots[k]
    for k in range(levels - 2, -1, -1):
        for i in range(tracers):
            values[i, k] = values[i, k] + ratios[k] * values[i, k + 1]
    z = lax.axis_index("gz")
    pair = [kept[i] for i in range(tracers)] + [kept[tracers]]
    top = [jnp.where((z == 1) | (z == 3), p, 0.0) for p in pair]
    low = [jnp.where((z == 0) | (z == 2), p, 0.0) for p in pair]
    top_gain = jnp.where(z == 2, 1.0, top[tracers])
    low_gain = jnp.where(z == 1, 1.0, low[tracers])
    for k in range(levels):
        gain[k] = low_gain * from_last[k] - top_gain * from_first[k]
        for i in range(tracers):
            base[i, k] = values[i, k] - top[i] * from_first[k] + low[i] * from_last[k]


def interface(upper, lower, tracers):
    heads, alpha, beta = upper[:tracers], upper[tracers], upper[tracers + 1]
    sums, rims, admit = lower[:tracers], lower[tracers : 2 * tracers], lower[2 * tracers]
    inverse = jnp.where(admit > 0.0, 1.0 / (admit + alpha), 0.0)
    flux = [(alpha * s + beta * r - admit * h) * inverse for s, r, h in zip(sums, rims, heads)]
    return flux, admit * alpha * inverse


def pair_kernel(own, other, merged, kept):
    tracers = kept.shape[0] - 1
    z = lax.axis_index("gz")
    lower_here = z % 2 == 1
    lower_pair = z >= 2
    upper, lower = [], []
    count = own.shape[0]
    for j in range(count):
        upper.append(jnp.where(lower_here, other[j], own[j]))
        lower.append(jnp.where(lower_here, own[j], other[j]))
    n = tracers + 2
    flux, gain = interface(upper[:n], lower[n:-1], tracers)
    across = jnp.where(lower_pair, upper[-1], lower[-1])
    gain = gain * across
    for i in range(tracers):
        kept[i] = flux[i]
    kept[tracers] = gain
    factor = across * jnp.where(lower_pair, upper[-2], lower[tracers])
    scale = 1.0 / (1.0 - factor * gain)
    for i in range(tracers):
        head = jnp.where(lower_pair, upper[n + i] + factor * flux[i], lower[i] - factor * flux[i])
        merged[i] = head * scale
    for i in range(tracers + 1):
        merged[tracers + i] = scale * (
            jnp.where(lower_pair, upper[n + tracers + i], lower[tracers + i] if i < 2 else 0.0)
        )


def final_kernel(own, other, base, gain, out, staged, sem):
    tracers, levels = base.shape[:2]
    lower_pair = lax.axis_index("gz") >= 2
    upper = [jnp.where(lower_pair, other[j], own[j]) for j in range(own.shape[0])]
    lower = [jnp.where(lower_pair, own[j], other[j]) for j in range(own.shape[0])]
    middle, _ = interface(upper[: tracers + 2], lower, tracers)
    for i in range(tracers):
        for k in range(levels):
            staged[i, k] = base[i, k] + middle[i] * gain[k]
        pltpu.make_async_copy(staged.at[i], out.at[i], sem).start()
    pltpu.make_async_copy(staged, out, sem).wait()


def local(
    tracer, east_flow, north_flow, vertical_flow, mixing_lateral, mixing_vertical, sea_mask, bottom
):
    tracers, levels, rows, width = tracer.shape
    arrays = tracers + 4
    tiles = len(slots_of(levels, width))
    assert arrays == 2 * GROUP
    plane = (rows, width)
    block = (levels, rows, width)
    ring = lax.axis_size("gx")
    cells = levels * rows * width
    near_pairs = [(i, i ^ 1) for i in range(ring)]
    far_pairs = [(i, (i + 1) % ring if i % 2 else (i - 1) % ring) for i in range(ring)]

    tracer_here, mixing, east, north, wet, vertical, mixing_down, west_tiles, east_tiles, to_far, to_near = call(
        pack_kernel,
        [tracer.shape] + [block] * 6 + [(arrays, tiles) + plane] * 2 + [(2, tiles) + plane] * 2,
        20 * cells,
        tracer, mixing_lateral, east_flow, north_flow, sea_mask, bottom, vertical_flow, mixing_vertical,
        in_specs=[HBM] * 8,
        scratch=[
            pltpu.VMEM(block, jnp.int32),
            pltpu.VMEM(plane, jnp.int32),
            pltpu.SemaphoreType.DMA((6,)),
        ],
    )
    far = lax.ppermute(to_far, "gx", far_pairs)
    near = lax.ppermute(to_near, "gx", near_pairs)
    far_tiles, far_moved, down, up, from_first, from_last, pivots, ratios, couplings, weights, rims = call(
        side_kernel,
        [(arrays, tiles) + plane, (len(moved_pairs(tracers)), tiles) + plane]
        + [block] * 7
        + [(2,) + block, (5,) + plane],
        50 * cells,
        wet, vertical, mixing_down, west_tiles, east_tiles,
    )
    lateral, sums, near_edges = call(
        interior_kernel,
        [tracer.shape, (2 * tracers,) + plane, (tracers, tiles) + plane],
        100 * cells,
        tracer_here, mixing, east, north, wet, weights, west_tiles, east_tiles, near,
    )
    edges, message = call(
        rim_kernel,
        [(tracers, tiles) + plane, (3 * tracers + 4,) + plane],
        20 * cells,
        far_tiles, far_moved, far, near_edges, lateral, weights, sums, rims,
    )
    other = lax.ppermute(message, "gz", [(i, i ^ 1) for i in range(4)])
    merged, kept = call(
        pair_kernel, [(2 * tracers + 1,) + plane, (tracers + 1,) + plane], cells, message, other
    )
    beyond = lax.ppermute(merged, "gz", [(i, i ^ 2) for i in range(4)])
    base, gain = call(
        block_kernel,
        [tracer.shape, block],
        40 * cells,
        lateral, edges, down, up, pivots, ratios, couplings, from_first, from_last, kept,
    )
    (result,) = call(
        final_kernel, [tracer.shape], 10 * cells, merged, beyond, base, gain,
        out_specs=[HBM],
        scratch=[pltpu.VMEM(tracer.shape, jnp.float32), pltpu.SemaphoreType.DMA],
    )
    return result


def solution(mesh):
    assert mesh.shape["gz"] == 4 and mesh.shape["gx"] % 2 == 0
    return jax.shard_map(
        local,
        mesh=mesh,
        in_specs=(
            P(None, "gz", None, "gx"),
            P("gz", None, "gx"),
            P("gz", None, "gx"),
            P("gz", None, "gx"),
            P("gz", None, "gx"),
            P("gz", None, "gx"),
            P("gz", None, "gx"),
            P(None, "gx"),
        ),
        out_specs=P(None, "gz", None, "gx"),
        check_vma=False,
    )
```
